32 devices in a mesh: fsdp: 16 (over z, y, core), sp: 2 (over x).
Axes of the slice: x: 2, y: 2, z: 4, core: 2. Of those that a mesh axis runs over, the one named last changes fastest.
Arguments:
- latent_tokens: bfloat16 [16, 1024, 1152], P('fsdp', 'sp'), may hold values from -6 to 6
- caption_tokens: bfloat16 [16, 120, 1152], P('fsdp', 'sp'), may hold values from -1.6953125 to 1.6953125
- caption_len: int32 [16], P('fsdp'), may hold values from 31 to 120, as said below
- time_embed: float32 [16, 6912], P('fsdp'), may hold values from -0.4 to 0.4
- mod_table: bfloat16 [6, 1152], P(None, 'fsdp'), may hold values from -0.3984375 to 0.3984375
- self_input_weight: bfloat16 [1152, 3456], P('fsdp'), may hold values from -0.1875 to 0.1875
- self_query_bias: bfloat16 [1152], P('fsdp'), may hold values from -0.5 to 0.5
- self_value_bias: bfloat16 [1152], P('fsdp'), may hold values from -0.5 to 0.5
- self_output_weight: bfloat16 [1152, 1152], P('fsdp'), may hold values from -1 to 1
- self_output_bias: bfloat16 [1152], P('fsdp'), may hold values from -0.5 to 0.5
- cross_query_weight: bfloat16 [1152, 1152], P('fsdp'), may hold values from -0.1875 to 0.1875
- cross_query_bias: bfloat16 [1152], P('fsdp'), may hold values from -0.5 to 0.5
- cross_keyval_weight: bfloat16 [1152, 2304], P('fsdp'), may hold values from -0.1875 to 0.1875
- cross_value_bias: bfloat16 [1152], P('fsdp'), may hold values from -0.5 to 0.5
- cross_output_weight: bfloat16 [1152, 1152], P('fsdp'), may hold values from -0.375 to 0.375
- cross_output_bias: bfloat16 [1152], P('fsdp'), may hold values from -0.5 to 0.5
- expand_weight: bfloat16 [1152, 4608], P('fsdp'), may hold values from -0.1875 to 0.1875
- expand_bias: bfloat16 [4608], P('fsdp'), may hold values from -0.5 to 0.5
- contract_weight: bfloat16 [4608, 1152], P('fsdp'), may hold values from -0.09375 to 0.09375
- contract_bias: bfloat16 [1152], P('fsdp'), may hold values from -0.5 to 0.5
- out_grad: bfloat16 [16, 1024, 1152], P('fsdp', 'sp'), may hold values from -6 to 6
Outputs:
- block_out: bfloat16 [16, 1024, 1152], P('fsdp', 'sp')
- latent_grad: float32 [16, 1024, 1152], P('fsdp', 'sp')
- caption_grad: float32 [16, 120, 1152], P('fsdp', 'sp')
- time_grad: float32 [16, 6912], P('fsdp')
- mod_table_grad: float32 [6, 1152], P(None, 'fsdp')
- self_input_weight_grad: float32 [1152, 3456], P('fsdp')
- self_query_bias_grad: float32 [1152], P('fsdp')
- self_value_bias_grad: float32 [1152], P('fsdp')
- self_output_weight_grad: float32 [1152, 1152], P('fsdp')
- self_output_bias_grad: float32 [1152], P('fsdp')
- cross_query_weight_grad: float32 [1152, 1152], P('fsdp')
- cross_query_bias_grad: float32 [1152], P('fsdp')
- cross_keyval_weight_grad: float32 [1152, 2304], P('fsdp')
- cross_value_bias_grad: float32 [1152], P('fsdp')
- cross_output_weight_grad: float32 [1152, 1152], P('fsdp')
- cross_output_bias_grad: float32 [1152], P('fsdp')
- expand_weight_grad: float32 [1152, 4608], P('fsdp')
- expand_bias_grad: float32 [4608], P('fsdp')
- contract_weight_grad: float32 [4608, 1152], P('fsdp')
- contract_bias_grad: float32 [1152], P('fsdp')
The draws below stay inside these ranges and needn't reach their ends.
Inputs may be any that keep to these rules, and one draw needn't show every extreme that they name: caption_len[b] is the number of leading caption tokens of latent b that are attended to; the rest are masked out.
All inputs are finite; a program needn't handle non-finite values.
Results may differ from the reference program's by a relative error of at most 0.025.
Values may be sent and summed in bfloat16 or wider, within the bound.
No kernel may reach another device: no remote copies, remote signals or barrier semaphores. Data moves between devices by JAX's collectives and lax.ppermute only.
A program may use at most 256 MiB of HBM per device.

```python
import math
import jax
import jax.numpy as jnp
from jax import lax

D = 1152
HEADS = 16
HEAD_DIM = 72
FF = 4608
CAP = 120
SEQ = 1024
LATENTS = 16


def draw_caption_len(key, part):
    least = CAP // 4 + 1
    drawn = jax.random.randint(key, (LATENTS,), least, CAP + 1)
    places = jnp.arange(LATENTS)
    drawn = jnp.where(places == 0, CAP, drawn)
    drawn = jnp.where(places == 1, least, drawn)
    return drawn.astype(jnp.int32)


def steps_of(own_key, shape, split, low, high):
    factor_of, own = 1.0, jax.random.fold_in(own_key, 6)
    for position, parts in split:
        heights = jnp.exp(jax.random.uniform(jax.random.fold_in(own, position), (parts,), jnp.float32, low / len(split), high / len(split)))
        factor_of = factor_of * jnp.repeat(heights, shape[position] // parts).reshape([-1 if axis == position else 1 for axis in range(len(shape))])
    return factor_of


def noise(stream_key, shape, scale, bound, split=(), dtype=jnp.bfloat16):
    array = jax.random.normal(stream_key, shape, jnp.float32) * scale
    if len(split) > 0:
        array = steps_of(stream_key, shape, split, -0.22, 0.18) * array
    return jnp.clip(array, min=-bound, max=bound).astype(dtype)


def setup_inputs(seed: int = 0) -> dict:
    keys = jax.random.split(jax.random.key(seed), 22)
    return {
        "latent_tokens": noise(keys[0], (LATENTS, SEQ, D), 1.0, 6.0, ((0, 16), (1, 2))),
        "caption_tokens": jnp.clip(jax.random.uniform(keys[1], (LATENTS, CAP, D), jnp.float32, -1.6953125, 1.6953125) * steps_of(keys[1], (LATENTS, CAP, D), ((0, 16), (1, 2)), -0.4, 0.0), -1.6953125, 1.6953125).astype(jnp.bfloat16),
        "caption_len": draw_caption_len(jax.random.fold_in(keys[21], 71), 0),
        "time_embed": jnp.clip(jax.random.uniform(keys[3], (LATENTS, 6 * D), jnp.float32, -0.4, 0.4) * steps_of(keys[3], (LATENTS, 6 * D), ((0, 16),), -0.4, 0.0), -0.4, 0.4),
        "mod_table": jnp.clip(jax.random.uniform(keys[4], (6, D), jnp.float32, -0.3984375, 0.3984375) * steps_of(keys[4], (6, D), ((1, 16),), -0.4, 0.0), -0.3984375, 0.3984375).astype(jnp.bfloat16),
        "self_input_weight": noise(keys[5], (D, 3 * D), D ** -0.5, 0.1875, ((0, 16),)),
        "self_query_bias": jnp.clip(jax.random.uniform(keys[6], (D,), jnp.float32, -0.5, 0.5) * steps_of(keys[6], (D,), ((0, 16),), -0.4, 0.0), -0.5, 0.5).astype(jnp.bfloat16),
        "self_value_bias": jnp.clip(jax.random.uniform(keys[7], (D,), jnp.float32, -0.5, 0.5) * steps_of(keys[7], (D,), ((0, 16),), -0.4, 0.0), -0.5, 0.5).astype(jnp.bfloat16),
        "self_output_weight": noise(keys[8], (D, D), (D // 32) ** -0.5, 1.0, ((0, 16),)),
        "self_output_bias": jnp.clip(jax.random.uniform(keys[9], (D,), jnp.float32, -0.5, 0.5) * steps_of(keys[9], (D,), ((0, 16),), -0.4, 0.0), -0.5, 0.5).astype(jnp.bfloat16),
        "cross_query_weight": noise(keys[10], (D, D), D ** -0.5, 0.1875, ((0, 16),)),
        "cross_query_bias": jnp.clip(jax.random.uniform(keys[11], (D,), jnp.float32, -0.5, 0.5) * steps_of(keys[11], (D,), ((0, 16),), -0.4, 0.0), -0.5, 0.5).astype(jnp.bfloat16),
        "cross_keyval_weight": noise(keys[12], (D, 2 * D), D ** -0.5, 0.1875, ((0, 16),)),
        "cross_value_bias": jnp.clip(jax.random.uniform(keys[13], (D,), jnp.float32, -0.5, 0.5) * steps_of(keys[13], (D,), ((0, 16),), -0.4, 0.0), -0.5, 0.5).astype(jnp.bfloat16),
        "cross_output_weight": noise(keys[14], (D, D), (D // 4) ** -0.5, 0.375, ((0, 16),)),
        "cross_output_bias": jnp.clip(jax.random.uniform(keys[15], (D,), jnp.float32, -0.5, 0.5) * steps_of(keys[15], (D,), ((0, 16),), -0.4, 0.0), -0.5, 0.5).astype(jnp.bfloat16),
        "expand_weight": noise(keys[16], (D, FF), D ** -0.5, 0.1875, ((0, 16),)),
        "expand_bias": jnp.clip(jax.random.uniform(keys[17], (FF,), jnp.float32, -0.5, 0.5) * steps_of(keys[17], (FF,), ((0, 16),), -0.4, 0.0), -0.5, 0.5).astype(jnp.bfloat16),
        "contract_weight": noise(keys[18], (FF, D), FF ** -0.5, 0.09375, ((0, 16),)),
        "contract_bias": jnp.clip(jax.random.uniform(keys[19], (D,), jnp.float32, -0.5, 0.5) * steps_of(keys[19], (D,), ((0, 16),), -0.4, 0.0), -0.5, 0.5).astype(jnp.bfloat16),
        "out_grad": noise(keys[20], (LATENTS, SEQ, D), 1.0, 6.0, ((0, 16), (1, 2))),
    }


HIGH = lax.Precision.HIGHEST
EPS = 1e-06
NEG = -1e+30

@jax.custom_vjp
def low(v):
    return lax.optimization_barrier(v.astype(jnp.bfloat16)).astype(jnp.float32)

@jax.custom_vjp
def low_back(v):
    return v

def low_keep(v):
    return (low(v), None)

def low_pass(kept, grad):
    return (grad,)

def back_keep(v):
    return (v, None)

def back_low(kept, grad):
    return (low(grad),)
low.defvjp(low_keep, low_pass)
low_back.defvjp(back_keep, back_low)

def modulated_norm(stream, shift, scale_rows):
    centre = stream - lax.optimization_barrier(jnp.mean(stream, axis=-1, keepdims=True))
    spread = lax.optimization_barrier(jnp.mean(centre * centre, axis=-1, keepdims=True))
    return centre * lax.rsqrt(spread + EPS) * (1.0 + scale_rows[:, None, :]) + shift[:, None, :]

def linear(inputs, weight):
    return jnp.einsum('lsd,de->lse', inputs, weight, precision=HIGH)

def softmax_rows(scores):
    row_peak = lax.optimization_barrier(jnp.max(scores, axis=-1, keepdims=True))
    exponent = jnp.exp(scores - row_peak)
    return exponent / lax.optimization_barrier(jnp.sum(exponent, axis=-1, keepdims=True))

def self_item(operands):
    queries, key_rows, value_rows = operands
    scores = low_back(jnp.einsum('qe,ke->qk', queries, key_rows, precision=HIGH) * HEAD_DIM ** (-0.5))
    weights_low = low(softmax_rows(scores))
    return jnp.einsum('qk,ke->qe', weights_low, value_rows, precision=HIGH)

def cross_latent(operands):
    queries, key_rows, value_rows, length = operands
    scores = low_back(jnp.einsum('she,che->hsc', queries, key_rows, precision=HIGH) * HEAD_DIM ** (-0.5))
    visible = jnp.arange(CAP) < length
    scores = jnp.where(visible[None, None, :], scores, NEG)
    weights_low = low(softmax_rows(scores))
    return jnp.einsum('hsc,che->she', weights_low, value_rows, precision=HIGH)

def head_items(tensor, latents):
    return tensor.reshape(latents, SEQ, HEADS, HEAD_DIM).transpose(0, 2, 1, 3).reshape(latents * HEADS, SEQ, HEAD_DIM)

def block_forward(params, stream, caption, lengths, embed):
    table, input_weight, query_bias, value_bias, output_weight, output_bias, xquery_weight, xquery_bias, keyval_weight, xvalue_bias, xoutput_weight, xoutput_bias, expand_weight, expand_bias, contract_weight, contract_bias = params
    latents = stream.shape[0]
    modulation = table[None] + embed.reshape(latents, 6, D)
    norm_one = low(modulated_norm(stream, modulation[:, 0], modulation[:, 1]))
    projected = linear(norm_one, input_weight)
    queries = low(low_back(projected[..., :D] + query_bias))
    key_rows = low(low_back(projected[..., D:2 * D]))
    value_rows = low(low_back(projected[..., 2 * D:] + value_bias))
    mixed_items = lax.map(jax.checkpoint(self_item), (head_items(queries, latents), head_items(key_rows, latents), head_items(value_rows, latents)))
    mixed_tokens = mixed_items.reshape(latents, HEADS, SEQ, HEAD_DIM).transpose(0, 2, 1, 3).reshape(latents, SEQ, D)
    mixed_tokens = low(low_back(mixed_tokens))
    attended = low_back(linear(mixed_tokens, output_weight) + output_bias)
    after_attn = stream + modulation[:, 2][:, None, :] * attended
    cross_queries = low(low_back(linear(low(after_attn), xquery_weight) + xquery_bias))
    keyval = linear(caption, keyval_weight)
    cross_keys = low(low_back(keyval[..., :D]))
    cross_values = low(low_back(keyval[..., D:] + xvalue_bias))
    cross_mixed = lax.map(jax.checkpoint(cross_latent), (cross_queries.reshape(latents, SEQ, HEADS, HEAD_DIM), cross_keys.reshape(latents, CAP, HEADS, HEAD_DIM), cross_values.reshape(latents, CAP, HEADS, HEAD_DIM), lengths))
    cross_mixed = low(low_back(cross_mixed.reshape(latents, SEQ, D)))
    crossed = low_back(linear(cross_mixed, xoutput_weight) + xoutput_bias)
    after_cross = after_attn + crossed
    norm_two = low(modulated_norm(after_cross, modulation[:, 3], modulation[:, 4]))
    hidden = low_back(linear(norm_two, expand_weight) + expand_bias)
    activated = low(jax.nn.gelu(hidden, approximate=True))
    fed = low_back(linear(activated, contract_weight) + contract_bias)
    return after_cross + modulation[:, 5][:, None, :] * fed

def reference(latent_tokens, caption_tokens, caption_len, time_embed, mod_table, self_input_weight, self_query_bias, self_value_bias, self_output_weight, self_output_bias, cross_query_weight, cross_query_bias, cross_keyval_weight, cross_value_bias, cross_output_weight, cross_output_bias, expand_weight, expand_bias, contract_weight, contract_bias, out_grad):
    params = tuple((item.astype(jnp.float32) for item in (mod_table, self_input_weight, self_query_bias, self_value_bias, self_output_weight, self_output_bias, cross_query_weight, cross_query_bias, cross_keyval_weight, cross_value_bias, cross_output_weight, cross_output_bias, expand_weight, expand_bias, contract_weight, contract_bias)))
    group = math.gcd(LATENTS, max(1, 4096 // SEQ))
    rounds = LATENTS // group

    def split_rows(tensor):
        return tensor.astype(jnp.float32).reshape((rounds, group) + tensor.shape[1:])
    slices = (split_rows(latent_tokens), split_rows(caption_tokens), caption_len.reshape(rounds, group), split_rows(time_embed), split_rows(out_grad))

    def accumulate(totals, data):
        stream, caption, lengths, embed, cotangent = data

        def forward(weights, stream_in, caption_in, embed_in):
            return block_forward(weights, stream_in, caption_in, lengths, embed_in)
        result, pullback = jax.vjp(forward, params, stream, caption, embed)
        weight_grads, stream_grad, caption_grad, embed_grad = pullback(cotangent)
        totals = jax.tree.map(lambda older, newer: older + newer, totals, weight_grads)
        return (totals, (result, stream_grad, caption_grad, embed_grad))
    zeros = tuple((jnp.zeros_like(item) for item in params))
    grads, (results, stream_grads, caption_grads, embed_grads) = lax.scan(accumulate, zeros, slices)
    block_out = results.reshape(LATENTS, SEQ, D).astype(jnp.bfloat16)
    latent_grad = stream_grads.reshape(LATENTS, SEQ, D)
    caption_grad = caption_grads.reshape(LATENTS, CAP, D)
    time_grad = embed_grads.reshape(LATENTS, 6 * D)
    return (block_out, latent_grad, caption_grad, time_grad, grads[0], grads[1], grads[2], grads[3], grads[4], grads[5], grads[6], grads[7], grads[8], grads[9], grads[10], grads[11], grads[12], grads[13], grads[14], grads[15])
```

```python
from functools import partial

import jax
import jax.numpy as jnp
from jax import lax
from jax.experimental import pallas as pl
from jax.experimental.pallas import tpu as pltpu
from jax.sharding import PartitionSpec as P

HEADS = 16
HD = 72
SCALE = HD**-0.5
EPS = 1e-06
NEG = -1e30
F32 = jnp.float32
BF = jnp.bfloat16
NT = (((1,), (1,)), ((), ()))
TN = (((0,), (0,)), ((), ()))
NN = (((1,), (0,)), ((), ()))
VMEM = 56 << 20


def dot(a, b, dims=NN):
    return lax.dot_general(a, b, dims, preferred_element_type=F32)


def self_fwd_kernel(q_ref, k_ref, v_ref, o_ref, lse_ref, *, heads):
    for h in range(heads):
        sl = slice(HD * h, HD * h + HD)
        q, k, v = q_ref[0, :, sl], k_ref[0, :, sl], v_ref[0, :, sl]
        s = dot(k, q, NT) * SCALE
        m = jnp.max(s, axis=0, keepdims=True)
        p = jnp.exp(s - m)
        total = jnp.sum(p, axis=0, keepdims=True)
        o = dot(v, p.astype(BF), TN) * (1.0 / total)
        o_ref[0, :, sl] = o.T.astype(BF)
        lse_ref[0, h : h + 1, :] = m + jnp.log(total)


def self_bwd_kernel(q_ref, k_ref, v_ref, g_ref, lse_ref, dq_ref, dk_ref, dv_ref, *, heads):
    for h in range(heads):
        sl = slice(HD * h, HD * h + HD)
        q, k, v, g = q_ref[0, :, sl], k_ref[0, :, sl], v_ref[0, :, sl], g_ref[0, :, sl]
        p = jnp.exp(dot(k, q, NT) * SCALE - lse_ref[0, h : h + 1, :])
        dp = dot(v, g, NT)
        delta = jnp.sum(p * dp, axis=0, keepdims=True)
        ds = (p * (dp - delta)).astype(BF)
        dv_ref[0, :, sl] = dot(p.astype(BF), g).astype(BF)
        dk_ref[0, :, sl] = (dot(ds, q) * SCALE).astype(BF)
        dq_ref[0, :, sl] = (dot(k, ds, TN) * SCALE).T.astype(BF)


def cross_fwd_kernel(q_ref, k_ref, v_ref, bias_ref, o_ref, lse_ref):
    for h in range(HEADS):
        sl = slice(HD * h, HD * h + HD)
        q, k, v = q_ref[0, :, sl], k_ref[0, :, sl], v_ref[0, :, sl]
        s = dot(k, q, NT) * SCALE + bias_ref[0]
        m = jnp.max(s, axis=0, keepdims=True)
        p = jnp.exp(s - m)
        total = jnp.sum(p, axis=0, keepdims=True)
        o = dot(v, p.astype(BF), TN) * (1.0 / total)
        o_ref[0, :, sl] = o.T.astype(BF)
        lse_ref[0, h : h + 1, :] = m + jnp.log(total)


def cross_bwd_kernel(q_ref, k_ref, v_ref, g_ref, bias_ref, lse_ref, dq_ref, dk_ref, dv_ref):
    for h in range(HEADS):
        sl = slice(HD * h, HD * h + HD)
        q, k, v, g = q_ref[0, :, sl], k_ref[0, :, sl], v_ref[0, :, sl], g_ref[0, :, sl]
        p = jnp.exp(dot(k, q, NT) * SCALE + bias_ref[0] - lse_ref[0, h : h + 1, :])
        dp = dot(v, g, NT)
        delta = jnp.sum(p * dp, axis=0, keepdims=True)
        ds = (p * (dp - delta)).astype(BF)
        dv_ref[0, :, sl] = dot(p.astype(BF), g).astype(BF)
        dk_ref[0, :, sl] = (dot(ds, q) * SCALE).astype(BF)
        dq_ref[0, :, sl] = (dot(k, ds, TN) * SCALE).T.astype(BF)


def per_latent(kernel, ins, outs, flops):
    def spec(shape):
        return pl.BlockSpec((1,) + tuple(shape[1:]), lambda i: (i, 0, 0))

    nbytes = sum(a.size * a.dtype.itemsize for a in ins)
    return pl.pallas_call(
        kernel,
        grid=(ins[0].shape[0],),
        in_specs=[spec(a.shape) for a in ins],
        out_specs=[spec(s) for s, _ in outs],
        out_shape=[jax.ShapeDtypeStruct(s, d) for s, d in outs],
        compiler_params=pltpu.CompilerParams(vmem_limit_bytes=VMEM),
        cost_estimate=pl.CostEstimate(flops=flops, bytes_accessed=2 * nbytes, transcendentals=0),
    )(*ins)


def self_forward(q, k, v):
    n, t, w = q.shape
    heads = w // HD
    return per_latent(
        partial(self_fwd_kernel, heads=heads),
        (q, k, v),
        [(q.shape, BF), ((n, heads, t), F32)],
        4 * n * heads * t * t * 256,
    )


def self_backward(q, k, v, g, lse):
    n, t, w = q.shape
    heads = w // HD
    return per_latent(
        partial(self_bwd_kernel, heads=heads),
        (q, k, v, g, lse),
        [(q.shape, BF)] * 3,
        10 * n * heads * t * t * 256,
    )


def cross_forward(q, k, v, bias):
    n, t, _ = q.shape
    return per_latent(
        cross_fwd_kernel, (q, k, v, bias), [(q.shape, BF), ((n, HEADS, t), F32)], 4 * n * HEADS * t * 128 * 256
    )


def cross_backward(q, k, v, g, bias, lse):
    n, t, _ = q.shape
    return per_latent(
        cross_bwd_kernel,
        (q, k, v, g, bias, lse),
        [(q.shape, BF), (k.shape, BF), (k.shape, BF)],
        10 * n * HEADS * t * 128 * 256,
    )


def swap(x):
    return lax.ppermute(x, "sp", [(0, 1), (1, 0)])


def pick(x, index, axis):
    return lax.dynamic_index_in_dim(x, index, axis, keepdims=False)


def gather_tokens(x, nsp):
    if nsp == 2:
        return jnp.concatenate([x, swap(x)], axis=1)
    return lax.all_gather(x, "sp", axis=1, tiled=True)


def scatter_tokens(x, nsp):
    if nsp == 2:
        half = x.shape[1] // 2
        return x[:, :half].astype(F32) + swap(x[:, half:].astype(BF)).astype(F32)
    return lax.psum_scatter(x.astype(BF), "sp", scatter_dimension=1, tiled=True).astype(F32)


def in_order(own, other, index, axis=-1):
    return jnp.where(
        index == 0, jnp.concatenate([own, other], axis=axis), jnp.concatenate([other, own], axis=axis)
    )


def halves(x, index, axis=-1):
    low, high = jnp.split(x, 2, axis=axis)
    return jnp.where(index == 0, low, high), jnp.where(index == 0, high, low)


def heads_to_tokens(x, nsp, index):
    if nsp == 2:
        half = x.shape[1] // 2
        return in_order(x[:, :half], swap(x[:, half:]), index)
    return lax.all_to_all(x, "sp", split_axis=1, concat_axis=2, tiled=True)


def tokens_to_heads(x, nsp, index):
    if nsp == 2:
        own, other = halves(x, index)
        return jnp.concatenate([own, swap(other)], axis=1)
    return lax.all_to_all(x, "sp", split_axis=2, concat_axis=1, tiled=True)


def gather_axis(x, nsp, index, axis):
    if nsp == 2:
        return in_order(x, swap(x), index, axis)
    return lax.all_gather(x, "sp", axis=axis, tiled=True)


def scatter_axis(x, nsp, index, axis):
    if nsp == 2:
        own, other = halves(x, index, axis)
        return own.astype(F32) + swap(other.astype(BF)).astype(F32)
    return lax.psum_scatter(x.astype(BF), "sp", scatter_dimension=axis, tiled=True).astype(F32)


def sum_sp(x, nsp):
    if nsp == 2:
        return x.astype(F32) + swap(x).astype(F32)
    return lax.psum(x, "sp").astype(F32)


def scatter_rows(x, nf):
    f = lax.axis_index("fsdp")
    core, y, z, nz = f % 2, (f // 2) % 2, f // 4, nf // 4
    _, rows, w = x.shape
    kind = x.dtype
    x = x.reshape(nz, 2, 2, rows, w)
    got = lax.ppermute(pick(x, 1 - core, 2), "fsdp", [(i, i ^ 1) for i in range(nf)])
    x = (pick(x, core, 2).astype(F32) + got.astype(F32)).astype(kind)
    got = lax.ppermute(pick(x, 1 - y, 1), "fsdp", [(i, i ^ 2) for i in range(nf)])
    x = (pick(x, y, 1).astype(F32) + got.astype(F32)).astype(kind)
    total = pick(x, z, 0).astype(F32)
    for d in range(1, nz):
        part = pick(x, (z + d) % nz, 0)
        total = total + lax.ppermute(part, "fsdp", [(i, (i + 4 * d) % nf) for i in range(nf)]).astype(F32)
    return total


def gather_rows(x):
    return lax.all_gather(x, "fsdp", axis=0, tiled=True)


def normalise(stream):
    centre = stream - jnp.mean(stream, axis=-1, keepdims=True)
    inverse = lax.rsqrt(jnp.mean(centre * centre, axis=-1, keepdims=True) + EPS)
    return centre * inverse, inverse


def norm_back(w, unit, inverse, scale):
    u = w * (1.0 + scale)
    stream = (
        u - jnp.mean(u, axis=-1, keepdims=True) - unit * jnp.mean(u * unit, axis=-1, keepdims=True)
    ) * inverse
    return stream, jnp.sum(w, axis=1), jnp.sum(w * unit, axis=1)


def linear(x, w):
    return jnp.einsum("lsd,de->lse", x, w, preferred_element_type=F32)


def linear_back(x, w):
    return jnp.einsum("lse,de->lsd", x, w, preferred_element_type=F32)


def weight_grad(x, g):
    return jnp.einsum("lsd,lse->de", x, g, preferred_element_type=F32).astype(BF)


def column_sum(x):
    return jnp.sum(x, axis=(0, 1), dtype=F32)


def on_device(
    latent_tokens,
    caption_tokens,
    caption_len,
    time_embed,
    mod_table,
    self_input_weight,
    self_query_bias,
    self_value_bias,
    self_output_weight,
    self_output_bias,
    cross_query_weight,
    cross_query_bias,
    cross_keyval_weight,
    cross_value_bias,
    cross_output_weight,
    cross_output_bias,
    expand_weight,
    expand_bias,
    contract_weight,
    contract_bias,
    out_grad,
):
    nsp, nf = lax.axis_size("sp"), lax.axis_size("fsdp")
    sp = lax.axis_index("sp")
    latents, local_len, width = latent_tokens.shape
    rows = width // nf
    own = width // nsp
    hidden_rows = contract_weight.shape[0]
    hidden_own = hidden_rows // nsp
    ff = hidden_rows * nf
    ff_own = ff // nsp

    input_shard = pick(self_input_weight.reshape(rows, 3, nsp, own), sp, 2).reshape(rows, 3 * own)
    keyval_shard = pick(cross_keyval_weight.reshape(rows, 2, nsp, own), sp, 2).reshape(rows, 2 * own)
    expand_shard = pick(expand_weight.reshape(rows, nf, nsp, hidden_own), sp, 2).reshape(rows, ff_own)
    contract_shard = pick(contract_weight.reshape(nsp, hidden_own, width), sp, 0)
    small = jnp.concatenate(
        [
            jnp.stack(
                [
                    self_query_bias,
                    self_value_bias,
                    self_output_bias,
                    cross_query_bias,
                    cross_value_bias,
                    cross_output_bias,
                    contract_bias,
                ]
            ),
            mod_table,
            expand_bias.reshape(rows, ff // width).T,
        ],
        axis=0,
    )
    smalls = small.shape[0]
    small = jnp.pad(small.T, ((0, 0), (0, 128 - smalls)))

    first = gather_rows(jnp.concatenate([input_shard, small], axis=1))
    whole_input = first[:, : 3 * own]
    smalls_all = first[:, 3 * own :].astype(F32).T
    second = gather_rows(
        jnp.concatenate(
            [self_output_weight, cross_query_weight, keyval_shard, cross_output_weight], axis=1
        )
    )
    whole_output = second[:, :width]
    whole_xquery = second[:, width : 2 * width]
    whole_keyval = second[:, 2 * width : 2 * width + 2 * own]
    whole_xoutput = second[:, 2 * width + 2 * own :]
    whole_expand = gather_rows(expand_shard)
    whole_contract = gather_rows(contract_shard)

    bias_query = pick(smalls_all[0].reshape(nsp, own), sp, 0)
    bias_value = pick(smalls_all[1].reshape(nsp, own), sp, 0)
    bias_output = smalls_all[2]
    bias_xquery = smalls_all[3]
    bias_xvalue = pick(smalls_all[4].reshape(nsp, own), sp, 0)
    bias_xoutput = smalls_all[5]
    bias_contract = smalls_all[6]
    table = smalls_all[7:13]
    bias_expand = smalls_all[13:smalls].T.reshape(nf, nsp, hidden_own)
    bias_expand = pick(bias_expand, sp, 1).reshape(ff_own)

    modulation = table[None] + time_embed.reshape(latents, 6, width)
    shift_a, scale_a, gate_a, shift_b, scale_b, gate_b = [
        modulation[:, i][:, None, :] for i in range(6)
    ]

    stream_all = gather_tokens(latent_tokens, nsp)
    grad_all = gather_tokens(out_grad, nsp)
    caption_all = gather_axis(caption_tokens, nsp, sp, 1)
    unit_all, _ = normalise(stream_all.astype(F32))
    norm_a = (unit_all * (1.0 + scale_a) + shift_a).astype(BF)
    projected = linear(norm_a, whole_input)
    queries = (projected[..., :own] + bias_query).astype(BF)
    keys = projected[..., own : 2 * own].astype(BF)
    values = (projected[..., 2 * own :] + bias_value).astype(BF)
    mixed, lse = self_forward(queries, keys, values)
    mixed_tokens = heads_to_tokens(mixed, nsp, sp)

    stream = latent_tokens.astype(F32)
    attended = linear(mixed_tokens, whole_output) + bias_output
    after_attn = stream + gate_a * attended
    attn_low = after_attn.astype(BF)

    cross_queries = (linear(attn_low, whole_xquery) + bias_xquery).astype(BF)
    keyval = linear(caption_all, whole_keyval)
    cross_keys = gather_axis(keyval[..., :own].astype(BF), nsp, sp, 2)
    cross_values = gather_axis((keyval[..., own:] + bias_xvalue).astype(BF), nsp, sp, 2)
    captions = caption_all.shape[1]
    place = jnp.arange(captions)
    bias = jnp.where(place[None] < caption_len[:, None], 0.0, NEG).astype(F32)[..., None]
    cross_mixed, cross_lse = cross_forward(cross_queries, cross_keys, cross_values, bias)
    crossed = linear(cross_mixed, whole_xoutput) + bias_xoutput
    after_cross = after_attn + crossed

    unit_b, inverse_b = normalise(after_cross)
    norm_b = gather_tokens((unit_b * (1.0 + scale_b) + shift_b).astype(BF), nsp)
    fed_grad = (gate_b * grad_all.astype(F32)).astype(BF)
    hidden = linear(norm_b, whole_expand) + bias_expand
    activated, gelu_back = jax.vjp(partial(jax.nn.gelu, approximate=True), hidden)
    activated = activated.astype(BF)
    hidden_grad = gelu_back(linear_back(fed_grad, whole_contract))[0].astype(BF)
    norm_b_grad = scatter_tokens(linear_back(hidden_grad, whole_expand), nsp)

    contract_wgrad = weight_grad(activated, fed_grad)
    expand_wgrad = weight_grad(norm_b, hidden_grad)
    fed = scatter_tokens(linear(activated, whole_contract), nsp) + bias_contract
    block_out = (after_cross + gate_b * fed).astype(BF)
    cotangent = out_grad.astype(F32)
    gate_b_grad = jnp.sum(cotangent * fed, axis=1)
    contract_bgrad = column_sum(fed_grad[:, :local_len] if nsp == 2 else gate_b * cotangent)
    expand_bgrad = column_sum(hidden_grad)

    cross_stream_grad, shift_b_grad, scale_b_grad = norm_back(norm_b_grad, unit_b, inverse_b, scale_b)
    cross_stream_grad = cross_stream_grad + cotangent
    crossed_grad = cross_stream_grad.astype(BF)
    xoutput_wgrad = weight_grad(cross_mixed, crossed_grad)
    xoutput_bgrad = column_sum(crossed_grad)
    cross_mixed_grad = linear_back(crossed_grad, whole_xoutput).astype(BF)
    xquery_grad, xkey_part, xvalue_part = cross_backward(
        cross_queries, cross_keys, cross_values, cross_mixed_grad, bias, cross_lse
    )
    attn_stream_grad = cross_stream_grad + linear_back(xquery_grad, whole_xquery)
    gate_a_grad = jnp.sum(attn_stream_grad * attended, axis=1)
    attended_grad = (gate_a * attn_stream_grad).astype(BF)
    mixed_grad = tokens_to_heads(linear_back(attended_grad, whole_output).astype(BF), nsp, sp)

    keyval_grad = jnp.concatenate(
        [scatter_axis(xkey_part, nsp, sp, 2), scatter_axis(xvalue_part, nsp, sp, 2)], axis=-1
    ).astype(BF)
    caption_grad = scatter_axis(linear_back(keyval_grad, whole_keyval), nsp, sp, 1)
    keyval_wgrad = weight_grad(caption_all, keyval_grad)
    xvalue_bgrad = column_sum(keyval_grad[..., own:])
    xquery_wgrad = weight_grad(attn_low, xquery_grad)
    xquery_bgrad = column_sum(xquery_grad)
    output_wgrad = weight_grad(mixed_tokens, attended_grad)
    output_bgrad = column_sum(attended_grad)

    query_grad, key_grad, value_grad = self_backward(queries, keys, values, mixed_grad, lse)
    projected_grad = jnp.concatenate([query_grad, key_grad, value_grad], axis=-1)
    input_wgrad = weight_grad(norm_a, projected_grad)
    query_bgrad = column_sum(query_grad)
    value_bgrad = column_sum(value_grad)
    norm_a_grad = scatter_tokens(linear_back(projected_grad, whole_input), nsp)
    unit_a, inverse_a = normalise(stream)
    stream_part, shift_a_grad, scale_a_grad = norm_back(norm_a_grad, unit_a, inverse_a, scale_a)
    latent_grad = attn_stream_grad + stream_part

    def owned(x):
        return scatter_rows(x.reshape(nf, x.shape[0] // nf, x.shape[1]), nf).astype(BF)

    contract_own, expand_own = owned(contract_wgrad), owned(expand_wgrad)
    keyval_own, input_own = owned(keyval_wgrad), owned(input_wgrad)
    output_own, xquery_own, xoutput_own = owned(output_wgrad), owned(xquery_wgrad), owned(xoutput_wgrad)

    def gather_sp(x):
        if nsp == 2:
            got = swap(x)
            return jnp.where(sp == 0, jnp.stack([x, got]), jnp.stack([got, x])).astype(F32)
        return lax.all_gather(x, "sp").astype(F32)

    contract_out = gather_sp(contract_own).reshape(hidden_rows, width)
    expand_out = (
        gather_sp(expand_own.reshape(rows, nf, hidden_own)).transpose(1, 2, 0, 3).reshape(rows, ff)
    )
    keyval_out = (
        gather_sp(keyval_own.reshape(rows, 2, own)).transpose(1, 2, 0, 3).reshape(rows, 2 * width)
    )
    input_out = (
        gather_sp(input_own.reshape(rows, 3, own)).transpose(1, 2, 0, 3).reshape(rows, 3 * width)
    )
    output_out, xquery_out, xoutput_out = [
        sum_sp(x, nsp) for x in (output_own, xquery_own, xoutput_own)
    ]

    def spread(x):
        return jnp.where(jnp.arange(nsp)[:, None] == sp, x[None], 0.0).reshape(nsp * x.shape[0])

    embed_part = jnp.stack(
        [shift_a_grad, scale_a_grad, gate_a_grad, shift_b_grad, scale_b_grad, gate_b_grad], axis=1
    )
    expand_bias_part = jnp.where(
        jnp.arange(nsp)[None, :, None] == sp, expand_bgrad.reshape(nf, 1, hidden_own), 0.0
    )
    vectors = [
        spread(query_bgrad),
        spread(value_bgrad),
        output_bgrad,
        xquery_bgrad,
        spread(xvalue_bgrad),
        xoutput_bgrad,
        contract_bgrad,
        expand_bias_part.reshape(ff),
    ]
    sizes = [v.shape[0] // nf for v in vectors]
    table_part = jnp.sum(embed_part, axis=0).reshape(6, nf, rows).transpose(1, 0, 2).reshape(nf, 6 * rows)
    vectors = jnp.concatenate([v.reshape(nf, -1) for v in vectors] + [table_part], axis=1)
    owned_small = sum_sp(scatter_rows(vectors[:, None, :], nf)[0], nsp)
    pieces, at = [], 0
    for size in sizes:
        pieces.append(owned_small[at : at + size])
        at += size
    table_out = owned_small[at:].reshape(6, rows)
    time_grad = sum_sp(embed_part.reshape(latents, 6 * width), nsp)
    return (
        block_out,
        latent_grad,
        caption_grad,
        time_grad,
        table_out,
        input_out,
        pieces[0],
        pieces[1],
        output_out,
        pieces[2],
        xquery_out,
        pieces[3],
        keyval_out,
        pieces[4],
        xoutput_out,
        pieces[5],
        expand_out,
        pieces[7],
        contract_out,
        pieces[6],
    )


def solution(mesh):
    row, vec, tokens = P("fsdp", None), P("fsdp"), P("fsdp", "sp", None)
    in_specs = (
        (tokens, tokens, vec, row, P(None, "fsdp"), row, vec, vec)
        + (row, vec) * 2
        + (row, vec) * 4
        + (tokens,)
    )
    out_specs = (
        (tokens, tokens, tokens, row, P(None, "fsdp"), row, vec, vec) + (row, vec) * 2 + (row, vec) * 4
    )
    return jax.shard_map(
        on_device, mesh=mesh, in_specs=in_specs, out_specs=out_specs, check_vma=False
    )
```

```python
from functools import partial

import jax
import jax.numpy as jnp
from jax import lax
from jax.experimental import pallas as pl
from jax.experimental.pallas import tpu as pltpu
from jax.sharding import PartitionSpec as P

HEADS = 16
HD = 72
GROUPS = 2
SCALE = HD**-0.5
COST = 1 << 20
EPS = 1e-06
NEG = -1e30
F32 = jnp.float32
BF = jnp.bfloat16
NT = (((1,), (1,)), ((), ()))
TN = (((0,), (0,)), ((), ()))
NN = (((1,), (0,)), ((), ()))
VMEM = 56 << 20


def dot(a, b, dims=NN):
    return lax.dot_general(a, b, dims, preferred_element_type=F32)


def whole(shape, n=1):
    return pl.BlockSpec((1,) + tuple(shape[1:]), lambda i, *_: (i,) + (0,) * (len(shape) - 1))


def constant(shape, at=None):
    at = at or (0,) * len(shape)
    return pl.BlockSpec(tuple(shape), lambda *_: at, pipeline_mode=pl.Buffered(1))


def anywhere(n):
    return [pl.BlockSpec(memory_space=pl.ANY)] * n


def smem():
    return pl.BlockSpec(memory_space=pltpu.SMEM)


def call(kernel, ins, in_specs, outs, out_specs, grid=(), scratch=(), waits=(), vmem=VMEM, aliases=None):
    n_in, n_wait = len(ins), len(waits)

    def body(*refs):
        kernel(*refs[:n_in], *refs[n_in + n_wait :])

    return pl.pallas_call(
        body,
        name=(kernel.func if isinstance(kernel, partial) else kernel).__name__,
        grid=grid,
        in_specs=list(in_specs) + anywhere(n_wait),
        out_specs=out_specs,
        out_shape=[jax.ShapeDtypeStruct(s, d) for s, d in outs],
        scratch_shapes=list(scratch),
        input_output_aliases=aliases or {},
        compiler_params=pltpu.CompilerParams(vmem_limit_bytes=vmem),
        cost_estimate=pl.CostEstimate(flops=0, bytes_accessed=COST, transcendentals=0),
    )(*ins, *waits)


def unit_of(v):
    centre = v - jnp.mean(v, axis=-1, keepdims=True)
    inverse = lax.rsqrt(jnp.mean(centre * centre, axis=-1, keepdims=True) + EPS)
    return centre * inverse, inverse


def qkv_kernel(x_ref, mod_ref, bias_ref, w_ref, norm_ref, qkv_ref):
    unit, _ = unit_of(x_ref[0].astype(F32))
    norm = (unit * (1.0 + mod_ref[0, 1:2]) + mod_ref[0, 0:1]).astype(BF)
    norm_ref[0] = norm
    qkv_ref[0] = (dot(norm, w_ref[:, : bias_ref.shape[1]]) + bias_ref[...]).astype(BF)


def qkv_forward(x, mods, bias, first, width3, waits=()):
    n, t, d = x.shape
    tb = min(256, t)
    rows = lambda w: pl.BlockSpec((1, tb, w), lambda i, j: (i, j, 0))
    return call(
        qkv_kernel,
        (x, mods, bias, first),
        [rows(d), whole(mods.shape), constant(bias.shape), constant(first.shape)],
        [((n, t, d), BF), ((n, t, width3), BF)],
        [rows(d), rows(width3)],
        grid=(n, t // tb),
        waits=waits,
    )


def self_fwd_kernel(qkv_ref, *refs, heads):
    o_ref, lse_ref = refs[-2:]
    for h in range(heads):
        q, k, v = [qkv_ref[0, :, (p * heads + h) * HD : (p * heads + h + 1) * HD] for p in range(3)]
        s = dot(k, q, NT) * SCALE
        m = jnp.max(s, axis=0, keepdims=True)
        p = jnp.exp(s - m)
        total = jnp.sum(p, axis=0, keepdims=True)
        o = dot(v, p.astype(BF), TN) * (1.0 / total)
        o_ref[0, :, h * HD : h * HD + HD] = o.T.astype(BF)
        lse_ref[0, h : h + 1, :] = m + jnp.log(total)


def self_forward(qkv, waits=()):
    n, t, w = qkv.shape
    heads = w // HD // 3
    outs = [((n, t, w // 3), BF), ((n, heads, t), F32)]
    return call(
        partial(self_fwd_kernel, heads=heads),
        (qkv,),
        [whole(qkv.shape)],
        outs,
        [whole(s) for s, _ in outs],
        grid=(n,),
        waits=waits,
        vmem=40 << 20,
    )


def middle_fwd_kernel(
    mixed_ref, x_ref, mod_ref, vec_ref, so_ref, xq_ref, xo_ref, k_ref, v_ref, mask_ref,
    attended_ref, low_ref, q_ref, lse_ref, cmix_ref, stream_ref, norm_ref,
):
    attended = dot(mixed_ref[0], so_ref[...]) + vec_ref[2:3]
    attended_ref[0] = attended.astype(BF)
    stream = x_ref[0].astype(F32) + mod_ref[0, 2:3] * attended
    low = stream.astype(BF)
    low_ref[0] = low
    q_ref[0] = (dot(low, xq_ref[...]) + vec_ref[3:4]).astype(BF)
    for h in range(HEADS):
        sl = slice(HD * h, HD * h + HD)
        q, k, v = q_ref[0, :, sl], k_ref[0, :, sl], v_ref[0, :, sl]
        s = dot(k, q, NT) * SCALE + mask_ref[0]
        m = jnp.max(s, axis=0, keepdims=True)
        p = jnp.exp(s - m)
        total = jnp.sum(p, axis=0, keepdims=True)
        o = dot(v, p.astype(BF), TN) * (1.0 / total)
        cmix_ref[0, :, sl] = o.T.astype(BF)
        lse_ref[0, h : h + 1, :] = m + jnp.log(total)
    stream = stream + dot(cmix_ref[0], xo_ref[...]) + vec_ref[5:6]
    stream_ref[0] = stream
    unit, _ = unit_of(stream)
    norm_ref[0] = (unit * (1.0 + mod_ref[0, 4:5]) + mod_ref[0, 3:4]).astype(BF)


def middle_forward(mixed, x, mods, vecs, second, k, v, mask, waits=()):
    n, t, d = x.shape
    tb = min(256, t)
    rows = lambda w: pl.BlockSpec((1, tb, w), lambda i, j: (i, j, 0))
    weight = lambda c: constant((d, d), (0, c))
    outs = [
        ((n, t, d), BF),
        ((n, t, d), BF),
        ((n, t, d), BF),
        ((n, HEADS, t), F32),
        ((n, t, d), BF),
        ((n, t, d), F32),
        ((n, t, d), BF),
    ]
    out_specs = [rows(d)] * 3 + [pl.BlockSpec((1, HEADS, tb), lambda i, j: (i, 0, j))] + [rows(d)] * 3
    return call(
        middle_fwd_kernel,
        (mixed, x, mods, vecs, second, second, second, k, v, mask),
        [rows(d), rows(d), whole(mods.shape), constant(vecs.shape), weight(0), weight(1), weight(2)]
        + [whole(k.shape), whole(v.shape), whole(mask.shape)],
        outs,
        out_specs,
        grid=(n, t // tb),
        waits=waits,
    )


ROOT = (2.0 / 3.141592653589793) ** 0.5


def ff_kernel(x_ref, g_ref, mod_ref, e_ref, *refs, parts):
    cs, (bias_ref, act_ref, hg_ref, fg_ref, out_ref, sum_ref, gsum_ref) = refs[:parts], refs[parts:]
    ff = bias_ref.shape[1]
    pw = ff // parts
    x = x_ref[0]
    fg = (mod_ref[0, 5:6] * g_ref[0].astype(F32)).astype(BF)
    fg_ref[0] = fg

    @pl.when(pl.program_id(1) == 0)
    def _():
        sum_ref[...] = jnp.zeros_like(sum_ref)
        gsum_ref[...] = jnp.zeros_like(gsum_ref)

    gsum_ref[0] += jnp.sum(fg.astype(F32), axis=0, keepdims=True)
    back = 0.0
    for j in range(parts):
        cols = slice(j * pw, (j + 1) * pw)
        h = dot(x, e_ref[:, cols]) + bias_ref[:, cols]
        u = dot(fg, cs[j][...], NT)
        square = h * h
        th = jnp.tanh(h * (ROOT + (ROOT * 0.044715) * square))
        half = 0.5 + 0.5 * th
        act_ref[0, :, cols] = (h * half).astype(BF)
        slope = half + h * (1.0 - th * th) * (0.5 * ROOT + (1.5 * ROOT * 0.044715) * square)
        hg = (u * slope).astype(BF)
        hg_ref[0, :, cols] = hg
        sum_ref[0, :, cols] += jnp.sum(hg.astype(F32), axis=0, keepdims=True)
        back = back + dot(hg, e_ref[:, cols], NT)
    out_ref[0] = back.astype(BF)


def feed_forward(x, g, mods, expand, contracts, bias, waits=()):
    n, t, d = x.shape
    ff, parts = bias.shape[0], len(contracts)
    tb = min(256, t)
    rows = lambda w: pl.BlockSpec((1, tb, w), lambda i, j: (i, j, 0))
    return call(
        partial(ff_kernel, parts=parts),
        (x, g, mods, expand, *[c for c, _ in contracts], bias.reshape(1, ff)),
        [rows(d), rows(d), whole(mods.shape), constant((d, ff))]
        + [constant((ff // parts, d), (0, b)) for _, b in contracts]
        + [constant((1, ff))],
        [((n, t, ff), BF)] * 2 + [((n, t, d), BF)] * 2 + [((n, 1, ff), F32), ((n, 1, d), F32)],
        [rows(ff), rows(ff), rows(d), rows(d), whole((n, 1, ff)), whole((n, 1, d))],
        grid=(n, t // tb),
        waits=waits,
        vmem=44 << 20,
    )


def fed_kernel(*refs, chunks, parts, steps):
    acts, cs, outs = refs[:chunks], refs[chunks : chunks + parts], refs[chunks + parts :]
    pw = cs[0].shape[0]
    for c in range(chunks):
        fed = sum(dot(acts[c][0, :, j * pw : (j + 1) * pw], cs[j][...]) for j in range(parts))
        outs[c][0] = fed.astype(BF)


def fed_forward(acts, contracts, d, waits=()):
    n, t, ff = acts[0].shape
    parts = len(contracts)
    tb = min(256, t)
    rows = lambda w: pl.BlockSpec((1, tb, w), lambda i, j: (i, j, 0))
    return call(
        partial(fed_kernel, chunks=len(acts), parts=parts, steps=t // tb),
        (*acts, *[c for c, _ in contracts]),
        [rows(ff)] * len(acts) + [constant((ff // parts, d), (0, b)) for _, b in contracts],
        [((n, t, d), BF)] * len(acts),
        [rows(d)] * len(acts),
        grid=(n, t // tb),
        waits=waits,
        vmem=32 << 20,
    )


def columns_kernel(*refs, chunks):
    lefts, rights, out_ref = refs[:chunks], refs[chunks : 2 * chunks], refs[-1]
    out_ref[...] = sum(dot(a[...], b[...], TN) for a, b in zip(lefts, rights)).astype(BF)


def columns_wgrad(lefts, rights, across, width, first, into=None, waits=()):
    flat = lambda x: x.reshape(-1, x.shape[-1])
    lefts, rights = [flat(x) for x in lefts], [flat(x) for x in rights]
    d = (rights if across else lefts)[0].shape[1]
    m, wide = lefts[0].shape[1], rights[0].shape[1]
    steps = (m if across else wide) // d
    if across:
        specs = [pl.BlockSpec((x.shape[0], d), lambda s: (0, s)) for x in lefts] + [constant(x.shape) for x in rights]
    else:
        specs = [constant(x.shape) for x in lefts] + [pl.BlockSpec((x.shape[0], d), lambda s: (0, s)) for x in rights]
    ins = [*lefts, *rights]
    aliases = {}
    if into is not None:
        waits = (into, *waits)
        aliases = {len(ins): 0}
    return call(
        partial(columns_kernel, chunks=len(lefts)),
        ins,
        specs,
        [((d, width), BF)],
        [pl.BlockSpec((d, d), lambda s: (0, first + s))],
        grid=(steps,),
        waits=waits,
        vmem=44 << 20,
        aliases=aliases,
    )[0]


def finish_kernel(fed_ref, got_ref, stream_ref, g_ref, mod_ref, vec_ref, out_ref, sum_ref):
    fed = fed_ref[0].astype(F32) + got_ref[0].astype(F32) + vec_ref[6:7]
    out_ref[0] = (stream_ref[0] + mod_ref[0, 5:6] * fed).astype(BF)
    sum_ref[0] = jnp.sum(g_ref[0].astype(F32) * fed, axis=0, keepdims=True)


def finish_forward(fed, got, stream, g, mods, vecs, waits=()):
    n, t, d = stream.shape
    return call(
        finish_kernel,
        (fed, got, stream, g, mods, vecs),
        [whole(stream.shape)] * 4 + [whole(mods.shape), constant(vecs.shape)],
        [((n, t, d), BF), ((n, 1, d), F32)],
        [whole(stream.shape), whole((n, 1, d))],
        grid=(n,),
        waits=waits,
    )


def norm_back(w, unit, inverse, scale):
    u = w * (1.0 + scale)
    stream = (
        u - jnp.mean(u, axis=-1, keepdims=True) - unit * jnp.mean(u * unit, axis=-1, keepdims=True)
    ) * inverse
    return stream, jnp.sum(w, axis=0, keepdims=True), jnp.sum(w * unit, axis=0, keepdims=True)


def middle_bwd_kernel(
    pos_ref, nb_ref, got_ref, stream_ref, g_ref, mod_ref, xo_ref, xq_ref, so_ref, k_ref, v_ref, mask_ref,
    q_ref, lse_ref, attended_ref,
    cg_ref, xg_ref, ag_ref, grad_ref, dk_ref, dv_ref, sum_ref, *refs,
):
    tg_refs, cm_ref = refs[:-1], refs[-1]
    step = pl.program_id(1)
    unit, inverse = unit_of(stream_ref[0])
    w = nb_ref[0].astype(F32) + got_ref[0].astype(F32)
    back, shift, scale = norm_back(w, unit, inverse, mod_ref[0, 4:5])
    grad = back + g_ref[0].astype(F32)
    crossed = grad.astype(BF)
    cg_ref[0] = crossed
    cm_ref[...] = dot(crossed, xo_ref[...], NT).astype(BF)

    @pl.when(step == 0)
    def _():
        dk_ref[...] = jnp.zeros_like(dk_ref)
        dv_ref[...] = jnp.zeros_like(dv_ref)
        sum_ref[...] = jnp.zeros_like(sum_ref)

    for h in range(HEADS):
        sl = slice(HD * h, HD * h + HD)
        q, k, v, g = q_ref[0, :, sl], k_ref[0, :, sl], v_ref[0, :, sl], cm_ref[:, sl]
        p = jnp.exp(dot(k, q, NT) * SCALE + mask_ref[0] - lse_ref[0, h : h + 1, :])
        dp = dot(v, g, NT)
        ds = (p * (dp - jnp.sum(p * dp, axis=0, keepdims=True))).astype(BF)
        dv_ref[0, :, sl] += dot(p.astype(BF), g)
        dk_ref[0, :, sl] += dot(ds, q) * SCALE
        xg_ref[0, :, sl] = (dot(k, ds, TN) * SCALE).T.astype(BF)
    grad = grad + dot(xg_ref[0], xq_ref[...], NT)
    grad_ref[0] = grad
    attended_grad = (mod_ref[0, 2:3] * grad).astype(BF)
    ag_ref[0] = attended_grad
    tokens_grad = dot(attended_grad, so_ref[...], NT).astype(BF)
    if len(tg_refs) == 2:
        half = tokens_grad.shape[1] // 2
        low, high = tokens_grad[:, :half], tokens_grad[:, half:]
        tg_refs[0][0] = jnp.where(pos_ref[0] == 0, low, high)
        tg_refs[1][0] = jnp.where(pos_ref[0] == 0, high, low)
    else:
        tg_refs[0][0] = tokens_grad
    sums = [
        shift,
        scale,
        jnp.sum(grad * attended_ref[0].astype(F32), axis=0, keepdims=True),
        jnp.sum(crossed.astype(F32), axis=0, keepdims=True),
        jnp.sum(xg_ref[0].astype(F32), axis=0, keepdims=True),
        jnp.sum(attended_grad.astype(F32), axis=0, keepdims=True),
    ]
    for i, total in enumerate(sums):
        sum_ref[0, i : i + 1] += total


def middle_backward(pos, nb, got, stream, g, mods, second, k, v, mask, q, lse, attended, nsp, waits=()):
    n, t, d = stream.shape
    tb = min(256, t)
    rows = lambda w: pl.BlockSpec((1, tb, w), lambda i, j: (i, j, 0))
    weight = lambda c: constant((d, d), (0, c))
    stats = pl.BlockSpec((1, HEADS, tb), lambda i, j: (i, 0, j))
    pieces = 2 if nsp == 2 else 1
    outs = [((n, t, d), BF)] * 3 + [((n, t, d), F32), (k.shape, F32), (v.shape, F32), ((n, 8, d), F32)]
    return call(
        middle_bwd_kernel,
        (pos, nb, got, stream, g, mods, second, second, second, k, v, mask, q, lse, attended),
        [smem()]
        + [rows(d)] * 4
        + [whole(mods.shape), weight(2), weight(1), weight(0), whole(k.shape), whole(v.shape), whole(mask.shape)]
        + [rows(d), stats, rows(d)],
        outs + [((n, t, d // pieces), BF)] * pieces,
        [rows(d)] * 4 + [whole(k.shape), whole(v.shape), whole((n, 8, d))] + [rows(d // pieces)] * pieces,
        grid=(n, t // tb),
        scratch=[pltpu.VMEM((tb, d), BF)],
        waits=waits,
        vmem=44 << 20,
    )


def self_bwd_kernel(qkv_ref, *refs, chunks, heads):
    gs, (lse_ref, grad_ref) = refs[:chunks], refs[chunks:]
    for h in range(heads):
        spans = [slice((p * heads + h) * HD, (p * heads + h + 1) * HD) for p in range(3)]
        q, k, v = [qkv_ref[0, :, sl] for sl in spans]
        g = jnp.concatenate([r[0, :, spans[0]] for r in gs], axis=0) if chunks > 1 else gs[0][0, :, spans[0]]
        p = jnp.exp(dot(k, q, NT) * SCALE - lse_ref[0, h : h + 1, :])
        dp = dot(v, g, NT)
        delta = jnp.sum(p * dp, axis=0, keepdims=True)
        ds = (p * (dp - delta)).astype(BF)
        grad_ref[0, :, spans[2]] = dot(p.astype(BF), g).astype(BF)
        grad_ref[0, :, spans[1]] = (dot(ds, q) * SCALE).astype(BF)
        grad_ref[0, :, spans[0]] = (dot(k, ds, TN) * SCALE).T.astype(BF)


def self_backward(qkv, gs, lse, waits=()):
    n, t, w = qkv.shape
    heads = w // HD // 3
    return call(
        partial(self_bwd_kernel, chunks=len(gs), heads=heads),
        (qkv, *gs, lse),
        [whole(qkv.shape)] + [whole(g.shape) for g in gs] + [whole(lse.shape)],
        [((n, t, w), BF)],
        [whole((n, t, w))],
        grid=(n,),
        waits=waits,
        vmem=40 << 20,
    )[0]


def input_bwd_kernel(*refs, chunks):
    gs, xs, w_ref = refs[:chunks], refs[chunks : 2 * chunks], refs[2 * chunks]
    outs, sum_ref = refs[2 * chunks + 1 : -1], refs[-1]

    @pl.when(pl.program_id(1) == 0)
    def _():
        sum_ref[...] = jnp.zeros_like(sum_ref)

    for c in range(chunks):
        value = dot(gs[c][0], w_ref[:, : gs[c].shape[2]], NT)
        outs[c][0] = value.astype(BF)
        unit, _ = unit_of(xs[c][0].astype(F32))
        sum_ref[0, 0:1] += jnp.sum(value, axis=0, keepdims=True)
        sum_ref[0, 1:2] += jnp.sum(value * unit, axis=0, keepdims=True)


def input_backward(grad, xs, first, waits=()):
    n, t, w = grad.shape
    d = first.shape[0]
    chunks = len(xs)
    each = t // chunks
    tb = min(256, each)
    blocks = each // tb
    rows = pl.BlockSpec((1, tb, d), lambda i, j: (i, j, 0))
    return call(
        partial(input_bwd_kernel, chunks=chunks),
        (*[grad] * chunks, *xs, first),
        [pl.BlockSpec((1, tb, w), lambda i, j, c=c: (i, c * blocks + j, 0)) for c in range(chunks)]
        + [rows] * chunks
        + [constant(first.shape)],
        [((n, each, d), BF)] * chunks + [((n, 8, d), F32)],
        [rows] * chunks + [whole((n, 8, d))],
        grid=(n, blocks),
        waits=waits,
        vmem=36 << 20,
    )


def last_kernel(w_ref, got_ref, x_ref, mod_ref, grad_ref, out_ref):
    unit, inverse = unit_of(x_ref[0].astype(F32))
    w = w_ref[0].astype(F32) + got_ref[0].astype(F32)
    u = w * (1.0 + mod_ref[0, 1:2])
    back = u - jnp.mean(u, axis=-1, keepdims=True) - unit * jnp.mean(u * unit, axis=-1, keepdims=True)
    out_ref[0] = grad_ref[0] + back * inverse


def last_backward(w, got, x, mods, grad, waits=()):
    n, t, d = x.shape
    tb = min(256, t)
    rows = pl.BlockSpec((1, tb, d), lambda i, j: (i, j, 0))
    return call(
        last_kernel,
        (w, got, x, mods, grad),
        [rows, rows, rows, whole(mods.shape), rows],
        [((n, t, d), F32)],
        [rows],
        grid=(n, t // tb),
        waits=waits,
        vmem=16 << 20,
    )[0]


def wgrad_kernel(pos_ref, *refs, pairs, extra, r):
    at = 0
    lefts, rights = [], []
    for a, b in pairs:
        lefts.append(refs[at : at + a])
        rights.append(refs[at + a : at + a + b])
        at += a + b
    extras = refs[at : at + extra]
    own_ref, other_ref = refs[at + extra :]
    first = pos_ref[1] == 0
    chips = own_ref.shape[0]

    def put(value, col):
        w = value.shape[1]
        for c in range(chips):
            low, high = value[2 * c * r : 2 * c * r + r], value[2 * c * r + r : 2 * c * r + 2 * r]
            own_ref[c, :, col : col + w] = jnp.where(first, low, high).astype(BF)
            other_ref[c, :, col : col + w] = jnp.where(first, high, low).astype(BF)

    col = 0
    for left, right in zip(lefts, rights):
        width = right[0].shape[1]
        for a in range(0, width, 1152):
            b = min(a + 1152, width)
            put(sum(dot(x[...], y[:, a:b], TN) for x, y in zip(left, right)), col + a)
        col += width
    if extra:
        pad = own_ref.shape[2] - 128 - col
        if pad:
            own_ref[:, :, col : col + pad] = jnp.zeros((chips, r, pad), BF)
            other_ref[:, :, col : col + pad] = jnp.zeros((chips, r, pad), BF)
        put(extras[0][...].astype(F32), own_ref.shape[2] - 128)


def wgrad(pos, pairs, nf, extra=None, waits=()):
    flat = lambda x: x.reshape(-1, x.shape[-1])
    pairs = [([flat(x) for x in a], [flat(x) for x in b]) for a, b in pairs]
    m = pairs[0][0][0].shape[1]
    r = m // nf
    cols = sum(b[0].shape[1] for _, b in pairs)
    if extra is not None:
        cols = -(-cols // 128) * 128 + 128
    ins = [x for a, b in pairs for x in a + b] + ([] if extra is None else [extra])
    shape = (nf // 2, r, cols)
    return call(
        partial(wgrad_kernel, pairs=[(len(a), len(b)) for a, b in pairs], extra=int(extra is not None), r=r),
        (pos, *ins),
        [smem()] + [pl.BlockSpec(memory_space=pltpu.VMEM)] * len(ins),
        [(shape, BF)] * 2,
        [pl.BlockSpec(memory_space=pltpu.VMEM)] * 2,
        waits=waits,
        vmem=40 << 20,
    )


def core_sum_kernel(pos_ref, own_ref, got_ref, y_ref, other_ref):
    first = pos_ref[2] == 0
    low = own_ref[0].astype(F32) + got_ref[0].astype(F32)
    high = own_ref[1].astype(F32) + got_ref[1].astype(F32)
    y_ref[0] = jnp.where(first, low, high).astype(BF)
    other_ref[0] = jnp.where(first, high, low).astype(BF)


def y_sum_kernel(pos_ref, own_ref, got_ref, *outs):
    nz = len(outs)
    for d in range(nz):
        at = lax.rem(pos_ref[3] + d, nz)
        outs[d][...] = (own_ref[at].astype(F32) + got_ref[at].astype(F32)).astype(BF)


def z_sum_kernel(*refs):
    refs[-1][...] = sum(x[...].astype(F32) for x in refs[:-1]).astype(BF)


def in_vmem(kernel, ins, outs, waits=()):
    spec = pl.BlockSpec(memory_space=pltpu.VMEM)
    specs = [smem() if x.dtype == jnp.int32 else spec for x in ins]
    return call(kernel, ins, specs, [(s, BF) for s in outs], [spec] * len(outs), waits=waits, vmem=16 << 20)


def shift_z(x, nf, d):
    return lax.ppermute(x, "fsdp", [(i, (i + 4 * d) % nf) for i in range(nf)])


def cross_y(x, nf):
    return lax.ppermute(x, "fsdp", [(i, i ^ 2) for i in range(nf)])


def cross_core(x, nf):
    return lax.ppermute(x, "fsdp", [(i, i ^ 1) for i in range(nf)])


def sum_core(pos, own, other, nf, waits=()):
    _, r, w = own.shape
    two, one = pl.BlockSpec((2, r, w), lambda i: (i, 0, 0)), pl.BlockSpec((1, r, w), lambda i: (i, 0, 0))
    return call(
        core_sum_kernel,
        (pos, own, cross_core(other, nf)),
        [smem(), two, two],
        [((nf // 4, r, w), BF)] * 2,
        [one, one],
        grid=(nf // 4,),
        waits=waits,
        vmem=16 << 20,
    )


def sum_y(pos, mine, other, nf, waits=()):
    nz, r, w = mine.shape
    return in_vmem(y_sum_kernel, (pos, mine, cross_y(other, nf)), [(r, w)] * nz, waits)


def sum_z(chunks, nf, waits=()):
    got = [shift_z(chunks[d], nf, d) for d in range(1, len(chunks))]
    return in_vmem(z_sum_kernel, (chunks[0], *got), [chunks[0].shape], waits)[0]


def swap(x):
    return lax.ppermute(x, "sp", [(0, 1), (1, 0)])


def pick(x, index, axis):
    return lax.dynamic_index_in_dim(x, index, axis, keepdims=False)


def in_order(own, other, index, axis=-1):
    return jnp.where(
        index == 0, jnp.concatenate([own, other], axis=axis), jnp.concatenate([other, own], axis=axis)
    )


def halves(x, index, axis=-1):
    low, high = jnp.split(x, 2, axis=axis)
    return jnp.where(index == 0, low, high), jnp.where(index == 0, high, low)


def gather_tokens(x, nsp):
    if nsp == 2:
        return [x, swap(x)]
    return [lax.all_gather(x, "sp", axis=1, tiled=True)]


def scatter_tokens(parts, nsp):
    if nsp == 2:
        return parts[0], swap(parts[1])
    total = lax.psum_scatter(parts[0], "sp", scatter_dimension=1, tiled=True)
    return total, jnp.zeros_like(total)


def heads_to_tokens(x, nsp, index, others):
    if nsp == 2:
        half = x.shape[1] // 2
        return in_order(x[:, :half], after(swap(x[:, half:]), *others), index)
    return lax.all_to_all(x, "sp", split_axis=1, concat_axis=2, tiled=True)


def tokens_to_heads(parts, nsp):
    if nsp == 2:
        return [parts[0], swap(parts[1])]
    return [lax.all_to_all(parts[0], "sp", split_axis=2, concat_axis=1, tiled=True)]


def gather_axis(x, nsp, index, axis):
    if nsp == 2:
        return in_order(x, swap(x), index, axis)
    return lax.all_gather(x, "sp", axis=axis, tiled=True)


def scatter_axis(x, nsp, index, axis):
    if nsp == 2:
        own, other = halves(x, index, axis)
        return own.astype(F32) + swap(other.astype(BF)).astype(F32)
    return lax.psum_scatter(x.astype(BF), "sp", scatter_dimension=axis, tiled=True).astype(F32)


def sum_sp(x, nsp):
    if nsp == 2:
        return x.astype(F32) + swap(x).astype(F32)
    return lax.psum(x, "sp").astype(F32)


def gather_sp(x, nsp, index):
    if nsp == 2:
        got = swap(x)
        return [jnp.where(index == 0, x, got).astype(F32), jnp.where(index == 0, got, x).astype(F32)]
    return list(lax.all_gather(x, "sp").astype(F32))


def merge_sp(x, sums, gathers, nsp, index):
    (a, b), (c, d) = sums[0], gathers[0]
    if nsp == 2:
        got = swap(x)
        total = x[:, a:b].astype(F32) + got[:, a:b].astype(F32)
        x, got = x[:, c:d].astype(F32), got[:, c:d].astype(F32)
        return total, [jnp.where(index == 0, x, got), jnp.where(index == 0, got, x)]
    return lax.psum(x[:, a:b].astype(F32), "sp"), list(lax.all_gather(x[:, c:d], "sp").astype(F32))


def copy_kernel(at_ref, *refs, n, dim):
    ins, out, sems = refs[:n], refs[n], refs[n + 1]
    copies = []
    for i in range(n):
        index = (slice(None),) * dim + (at_ref[i],)
        copies.append(pltpu.make_async_copy(ins[i], out.at[index], sems.at[i]))
    for c in copies:
        c.start()
    for c in copies:
        c.wait()


def place_all(parts, at, dim, waits=()):
    n = len(parts)
    shape = parts[0].shape[:dim] + (n,) + parts[0].shape[dim:]
    return call(
        partial(copy_kernel, n=n, dim=dim),
        (at, *parts),
        [smem()] + anywhere(n),
        [(shape, parts[0].dtype)],
        [pl.BlockSpec(memory_space=pltpu.VMEM)],
        scratch=[pltpu.SemaphoreType.DMA((n,))],
        waits=waits,
        vmem=24 << 20,
    )[0]


def after(x, *others):
    return lax.optimization_barrier((x, *others))[0]


def column_sum(x):
    return jnp.sum(x, axis=(0, 1), dtype=F32)


def linear(x, w):
    return jnp.einsum("lsd,de->lse", x, w, preferred_element_type=F32)


def linear_back(x, w):
    return jnp.einsum("lse,de->lsd", x, w, preferred_element_type=F32)


def on_device(
    latent_tokens,
    caption_tokens,
    caption_len,
    time_embed,
    mod_table,
    self_input_weight,
    self_query_bias,
    self_value_bias,
    self_output_weight,
    self_output_bias,
    cross_query_weight,
    cross_query_bias,
    cross_keyval_weight,
    cross_value_bias,
    cross_output_weight,
    cross_output_bias,
    expand_weight,
    expand_bias,
    contract_weight,
    contract_bias,
    out_grad,
):
    nsp, nf = lax.axis_size("sp"), lax.axis_size("fsdp")
    sp, fsdp = lax.axis_index("sp"), lax.axis_index("fsdp")
    core, y, z, nz = fsdp % 2, (fsdp // 2) % 2, fsdp // 4, nf // 4
    pos = jnp.stack([sp, core, y, z]).astype(jnp.int32)
    latents, local_len, width = latent_tokens.shape
    rows = width // nf
    own = width // nsp
    hidden_rows = contract_weight.shape[0]
    hidden_own = hidden_rows // nsp
    parts = max(1, hidden_own // rows)
    block = hidden_own // parts
    part_width = nf * block

    def columns(w, pieces, groups=1):
        size = w.shape[1] // pieces // nsp // groups
        out = []
        for i in range(nsp):
            starts = [
                p * size * nsp * groups + (i * groups + g) * size for g in range(groups) for p in range(pieces)
            ]
            out.append(jnp.concatenate([w[:, a : a + size] for a in starts], axis=1))
        if nsp == 2:
            return jnp.where(sp == 0, out[0], out[1])
        return pick(jnp.stack(out), sp, 0)

    small = jnp.concatenate(
        [
            jnp.stack(
                [
                    self_query_bias,
                    self_value_bias,
                    self_output_bias,
                    cross_query_bias,
                    cross_value_bias,
                    cross_output_bias,
                    contract_bias,
                ]
            ),
            mod_table,
            expand_bias.reshape(-1, rows),
        ],
        axis=0,
    )
    smalls = small.shape[0]
    small = jnp.pad(small.T, ((0, 0), (0, 128 - smalls)))

    stream_swap = gather_tokens(latent_tokens, nsp)

    grads = gather_tokens(out_grad, nsp)
    caption_all = gather_axis(caption_tokens, nsp, sp, 1)
    stream_all = jnp.concatenate(stream_swap, axis=1)
    first = jnp.concatenate([columns(self_input_weight, 3), small], axis=1)
    second = jnp.concatenate(
        [self_output_weight, cross_query_weight, cross_output_weight, columns(cross_keyval_weight, 2)], axis=1
    )
    last = pick(expand_weight.reshape(rows, nf, nsp, parts, block), sp, 2)
    last = last.transpose(0, 2, 1, 3).reshape(rows, parts * part_width)
    contract_shard = pick(contract_weight.reshape(nsp, parts, block, width), sp, 0)
    if block == rows:
        last = jnp.concatenate([last] + [contract_shard[j] for j in range(parts)], axis=1)

    second = lax.all_gather(second, "fsdp", axis=0, tiled=True)
    ring = [first] + [shift_z(first, nf, d) for d in range(1, nz)]
    across = [cross_y(x, nf) for x in ring]
    at = jnp.stack([((z - d) % nz) * 2 + y for d in range(nz)] + [((z - d) % nz) * 2 + 1 - y for d in range(nz)])
    mine = place_all(ring + across, at.astype(jnp.int32), 0, (stream_all, last, caption_all))
    first = place_all([mine, cross_core(mine, nf)], jnp.stack([core, 1 - core]).astype(jnp.int32), 1)
    first = first.reshape(width, -1)
    whole_expand = lax.all_gather(after(last, mine), "fsdp", axis=0, tiled=True)
    if block == rows:
        whole_contracts = [(whole_expand, parts * part_width // width + j) for j in range(parts)]
    else:
        contract_shard = lax.all_gather(after(contract_shard[0], mine), "fsdp", axis=0, tiled=True)
        whole_contracts = [(contract_shard, 0)]

    smalls_all = first[:, 3 * own :].astype(F32).T

    def own_part(v):
        return pick(v.reshape(nsp, own), sp, 0)

    bias_query, bias_value = own_part(smalls_all[0]), own_part(smalls_all[1])
    bias_qkv = jnp.concatenate([bias_query, jnp.zeros_like(bias_query), bias_value]).reshape(1, 3 * own)
    vecs = smalls_all[:8]
    bias_xvalue = own_part(smalls_all[4])
    bias_expand = smalls_all[13:smalls].reshape(-1, nf, rows).transpose(1, 0, 2).reshape(nf, nsp, parts, block)
    bias_expand = pick(bias_expand, sp, 1).transpose(1, 0, 2).reshape(parts * part_width)
    mods = smalls_all[7:13][None] + time_embed.reshape(latents, 6, width)
    mods = jnp.pad(mods, ((0, 0), (0, 2), (0, 0)))

    norm_a, qkv = qkv_forward(stream_all, mods, bias_qkv, first, 3 * own)

    mixed, lse = self_forward(qkv, tuple(grads[1:]))
    second = after(second, mixed)
    whole_keyval = second[:, 3 * width :]

    keyval = linear(caption_all, whole_keyval)
    cross_keys = gather_axis(keyval[..., :own].astype(BF), nsp, sp, 2)
    cross_values = gather_axis((keyval[..., own:] + bias_xvalue).astype(BF), nsp, sp, 2)
    mixed_tokens = heads_to_tokens(mixed, nsp, sp, (cross_keys, cross_values))
    place = jnp.arange(caption_all.shape[1])
    mask = jnp.where(place[None] < caption_len[:, None], 0.0, NEG).astype(F32)[..., None]
    attended, attn_low, cross_queries, cross_lse, cross_mixed, after_cross, norm_b = middle_forward(
        mixed_tokens, latent_tokens, mods, vecs, second, cross_keys, cross_values, mask
    )

    norm_bs = gather_tokens(norm_b, nsp)
    ff_out = [None] * len(norm_bs)
    waits = ()
    for c in reversed(range(len(norm_bs))):
        ff_out[c] = feed_forward(norm_bs[c], grads[c], mods, whole_expand, whole_contracts, bias_expand, waits)
        waits = (ff_out[c][3],)
    acts, hidden_grads, fed_grads, norm_b_grads, hidden_sums, fed_sums = zip(*ff_out)
    norm_b_terms = scatter_tokens(norm_b_grads, nsp)
    expand_bgrad = sum(jnp.sum(x, axis=(0, 1)) for x in hidden_sums)
    if nsp == 2:
        contract_bgrad = jnp.sum(fed_sums[0], axis=(0, 1))
    else:
        contract_bgrad = column_sum(mods[:, 5:6] * out_grad.astype(F32))
    if block == rows:
        ff_own = columns_wgrad(acts, fed_grads, True, 2 * parts * width, 0)
        ff_own = columns_wgrad(norm_bs, hidden_grads, False, 2 * parts * width, parts, ff_own, (norm_b_terms[1],))
        ff_done = ff_own
        ff_own = lax.psum_scatter(ff_own, "fsdp", scatter_dimension=0, tiled=True)
        ff_sp = gather_sp(ff_own, nsp, sp)
        contract_sp, expand_sp = [g[:, : parts * width] for g in ff_sp], [g[:, parts * width :] for g in ff_sp]
    else:
        contract_own = jnp.einsum("lsd,lse->de", acts[0], fed_grads[0], preferred_element_type=F32).astype(BF)
        expand_own = jnp.einsum("lsd,lse->de", norm_bs[0], hidden_grads[0], preferred_element_type=F32).astype(BF)
        ff_done = expand_own
        contract_sp = gather_sp(lax.psum_scatter(contract_own, "fsdp", scatter_dimension=0, tiled=True), nsp, sp)
        expand_sp = gather_sp(lax.psum_scatter(expand_own, "fsdp", scatter_dimension=0, tiled=True), nsp, sp)

    crossed_grad, xquery_grad, attended_grad, attn_stream_grad, dk, dv, sums, *tokens_grads = middle_backward(
        pos, *norm_b_terms, after_cross, out_grad, mods, second, cross_keys, cross_values, mask,
        cross_queries, cross_lse, attended, nsp, waits=(ff_done,),
    )
    shift_b_grad, scale_b_grad, gate_a_grad = sums[:, 0], sums[:, 1], sums[:, 2]
    mixed_grads = tokens_to_heads(tokens_grads, nsp)
    cross_halves = wgrad(pos, [([attn_low], [xquery_grad]), ([cross_mixed], [crossed_grad])], nf)
    feds = fed_forward(acts, whole_contracts, width, (cross_halves[0],))
    cross_core_sum = sum_core(pos, *cross_halves, nf, waits=(feds[0],))

    keyval_grad = jnp.concatenate([scatter_axis(dk, nsp, sp, 2), scatter_axis(dv, nsp, sp, 2)], axis=-1).astype(BF)
    middle_halves = wgrad(
        pos, [([mixed_tokens], [attended_grad]), ([caption_all], [keyval_grad])], nf, waits=(cross_core_sum[0], mixed_grads[-1])
    )
    middle_core = sum_core(pos, *middle_halves, nf)
    caption_grad = scatter_axis(linear_back(keyval_grad, whole_keyval), nsp, sp, 1)
    xvalue_bgrad = column_sum(keyval_grad[..., own:])

    projected_grad = self_backward(qkv, mixed_grads, lse, (cross_core_sum[0], middle_core[0]))
    cross_y_sum = sum_y(pos, *cross_core_sum, nf, waits=(projected_grad,))
    input_out = input_backward(projected_grad, stream_swap, first, (cross_y_sum[0],))
    norm_a_terms = scatter_tokens(list(input_out[:-1]), nsp)
    shift_a_grad, scale_a_grad = input_out[-1][:, 0], input_out[-1][:, 1]
    fed_terms = scatter_tokens(feds, nsp)
    block_out, gate_b_grad = finish_forward(
        *fed_terms, after_cross, out_grad, mods, vecs, waits=(projected_grad,)
    )
    gate_b_grad = gate_b_grad[:, 0]

    def spread(x):
        return jnp.where(jnp.arange(nsp)[:, None] == sp, x[None], 0.0).reshape(nsp * x.shape[0])

    qkv_bgrad = column_sum(projected_grad)
    expand_bias_part = jnp.where(
        jnp.arange(nsp)[None, :, None, None] == sp,
        expand_bgrad.reshape(parts, nf, block).transpose(1, 0, 2)[:, None],
        0.0,
    ).reshape(nf, -1, rows)
    vectors = jnp.stack(
        [
            spread(qkv_bgrad[:own]),
            spread(qkv_bgrad[2 * own :]),
            jnp.sum(sums[:, 5], axis=0),
            jnp.sum(sums[:, 4], axis=0),
            spread(xvalue_bgrad),
            jnp.sum(sums[:, 3], axis=0),
            contract_bgrad,
            jnp.sum(shift_a_grad, axis=0),
            jnp.sum(scale_a_grad, axis=0),
            jnp.sum(gate_a_grad, axis=0),
            jnp.sum(shift_b_grad, axis=0),
            jnp.sum(scale_b_grad, axis=0),
            jnp.sum(gate_b_grad, axis=0),
        ]
    )
    vectors = jnp.concatenate([vectors, expand_bias_part.transpose(1, 0, 2).reshape(-1, width)])
    count = vectors.shape[0]
    vectors = jnp.pad(vectors.T, ((0, 0), (0, 128 - count))).astype(BF)
    middle_y = sum_y(pos, *middle_core, nf, waits=(block_out,))
    input_halves = wgrad(pos, [([norm_a], [projected_grad])], nf, extra=vectors, waits=(middle_y[0],))
    contract_out = jnp.concatenate(
        [g[:, j * width : (j + 1) * width] for g in contract_sp for j in range(contract_sp[0].shape[1] // width)], axis=0
    )
    expand_out = jnp.stack(
        [g.reshape(rows, parts, nf, block).transpose(0, 2, 1, 3) for g in expand_sp], axis=2
    ).reshape(rows, -1)
    input_core = sum_core(pos, *input_halves, nf)
    cross_own = sum_z(cross_y_sum, nf, waits=(input_core[0],))
    latent_grad = last_backward(*norm_a_terms, latent_tokens, mods, attn_stream_grad, (cross_own,))
    middle_own = sum_z(middle_y, nf, waits=(latent_grad, contract_out, expand_out))
    input_y = sum_y(pos, *input_core, nf, waits=(middle_own,))

    cross_sum = sum_sp(cross_own, nsp)
    xquery_out, xoutput_out = cross_sum[:, :width], cross_sum[:, width:]
    output_out, keyvals = merge_sp(middle_own, [(0, width)], [(width, width + 2 * own)], nsp, sp)
    keyval_out = jnp.concatenate([g[:, p * own : (p + 1) * own] for p in range(2) for g in keyvals], axis=1)
    input_own = sum_z(input_y, nf, waits=(xquery_out, xoutput_out, output_out, keyval_out))
    owned, inputs = merge_sp(
        input_own, [(input_own.shape[1] - 128, input_own.shape[1])], [(0, 3 * own)], nsp, sp
    )
    input_out = jnp.concatenate([g[:, p * own : (p + 1) * own] for p in range(3) for g in inputs], axis=1)
    owned = owned[:, :count].T
    expand_bout = owned[13:count].reshape(hidden_rows)

    embed_part = jnp.stack(
        [shift_a_grad, scale_a_grad, gate_a_grad, shift_b_grad, scale_b_grad, gate_b_grad], axis=1
    )
    time_grad = sum_sp(embed_part.reshape(latents, 6 * width), nsp)
    table_out = owned[7:13]
    return (
        block_out,
        latent_grad,
        caption_grad,
        time_grad,
        table_out,
        input_out,
        owned[0],
        owned[1],
        output_out,
        owned[2],
        xquery_out,
        owned[3],
        keyval_out,
        owned[4],
        xoutput_out,
        owned[5],
        expand_out,
        expand_bout,
        contract_out,
        owned[6],
    )


def solution(mesh):
    row, vec, tokens = P("fsdp", None), P("fsdp"), P("fsdp", "sp", None)
    in_specs = (
        (tokens, tokens, vec, row, P(None, "fsdp"), row, vec, vec)
        + (row, vec) * 2
        + (row, vec) * 4
        + (tokens,)
    )
    out_specs = (
        (tokens, tokens, tokens, row, P(None, "fsdp"), row, vec, vec) + (row, vec) * 2 + (row, vec) * 4
    )
    return jax.shard_map(
        on_device, mesh=mesh, in_specs=in_specs, out_specs=out_specs, check_vma=False
    )
```

```python
from functools import partial

import jax
import jax.numpy as jnp
from jax import lax
from jax.experimental import pallas as pl
from jax.experimental.pallas import tpu as pltpu
from jax.sharding import PartitionSpec as P

HEADS = 16
HD = 72
GROUPS = 2
SCALE = HD**-0.5
COST = 1 << 20
EPS = 1e-06
NEG = -1e30
F32 = jnp.float32
BF = jnp.bfloat16
NT = (((1,), (1,)), ((), ()))
TN = (((0,), (0,)), ((), ()))
NN = (((1,), (0,)), ((), ()))
VMEM = 56 << 20


def dot(a, b, dims=NN):
    return lax.dot_general(a, b, dims, preferred_element_type=F32)


def whole(shape, n=1):
    return pl.BlockSpec((1,) + tuple(shape[1:]), lambda i, *_: (i,) + (0,) * (len(shape) - 1))


def constant(shape, at=None):
    at = at or (0,) * len(shape)
    return pl.BlockSpec(tuple(shape), lambda *_: at, pipeline_mode=pl.Buffered(1))


def anywhere(n):
    return [pl.BlockSpec(memory_space=pl.ANY)] * n


def smem():
    return pl.BlockSpec(memory_space=pltpu.SMEM)


def call(kernel, ins, in_specs, outs, out_specs, grid=(), scratch=(), waits=(), vmem=VMEM, aliases=None, token=False):
    n_in, n_wait = len(ins), len(waits)
    if token:
        outs, out_specs = [*outs, ((8, 128), F32)], [*out_specs, pl.BlockSpec((8, 128), lambda *_: (0, 0))]

    def body(*refs):
        if token:
            at = n_in + n_wait + len(outs) - 1
            refs[at][...] = jnp.zeros((8, 128), F32)
            refs = refs[:at] + refs[at + 1 :]
        kernel(*refs[:n_in], *refs[n_in + n_wait :])

    return pl.pallas_call(
        body,
        name=(kernel.func if isinstance(kernel, partial) else kernel).__name__,
        grid=grid,
        in_specs=list(in_specs) + anywhere(n_wait),
        out_specs=out_specs,
        out_shape=[jax.ShapeDtypeStruct(s, d) for s, d in outs],
        scratch_shapes=list(scratch),
        input_output_aliases=aliases or {},
        compiler_params=pltpu.CompilerParams(vmem_limit_bytes=vmem),
        cost_estimate=pl.CostEstimate(flops=0, bytes_accessed=COST, transcendentals=0),
    )(*ins, *waits)


def unit_of(v):
    centre = v - jnp.mean(v, axis=-1, keepdims=True)
    inverse = lax.rsqrt(jnp.mean(centre * centre, axis=-1, keepdims=True) + EPS)
    return centre * inverse, inverse


def qkv_kernel(x_ref, mod_ref, bias_ref, w_ref, norm_ref, qkv_ref):
    unit, _ = unit_of(x_ref[0].astype(F32))
    norm = (unit * (1.0 + mod_ref[0, 1:2]) + mod_ref[0, 0:1]).astype(BF)
    norm_ref[0] = norm
    qkv_ref[0] = (dot(norm, w_ref[:, : bias_ref.shape[1]]) + bias_ref[...]).astype(BF)


def qkv_forward(x, mods, bias, first, width3, waits=()):
    n, t, d = x.shape
    tb = min(256, t)
    rows = lambda w: pl.BlockSpec((1, tb, w), lambda i, j: (i, j, 0))
    return call(
        qkv_kernel,
        (x, mods, bias, first),
        [rows(d), whole(mods.shape), constant(bias.shape), constant(first.shape)],
        [((n, t, d), BF), ((n, t, width3), BF)],
        [rows(d), rows(width3)],
        grid=(n, t // tb),
        waits=waits,
    )


def self_fwd_kernel(qkv_ref, *refs, heads):
    o_ref, lse_ref = refs[-2:]
    for h in range(heads):
        q, k, v = [qkv_ref[0, :, (p * heads + h) * HD : (p * heads + h + 1) * HD] for p in range(3)]
        s = dot(k, q, NT) * SCALE
        m = jnp.max(s, axis=0, keepdims=True)
        p = jnp.exp(s - m)
        total = jnp.sum(p, axis=0, keepdims=True)
        o = dot(v, p.astype(BF), TN) * (1.0 / total)
        o_ref[0, :, h * HD : h * HD + HD] = o.T.astype(BF)
        lse_ref[0, h : h + 1, :] = m + jnp.log(total)


def self_forward(qkv, waits=()):
    n, t, w = qkv.shape
    heads = w // HD // 3
    outs = [((n, t, w // 3), BF), ((n, heads, t), F32)]
    return call(
        partial(self_fwd_kernel, heads=heads),
        (qkv,),
        [whole(qkv.shape)],
        outs,
        [whole(s) for s, _ in outs],
        grid=(n,),
        waits=waits,
        vmem=40 << 20,
    )


def middle_fwd_kernel(
    mixed_ref, x_ref, mod_ref, vec_ref, so_ref, xq_ref, xo_ref, k_ref, v_ref, mask_ref,
    attended_ref, low_ref, q_ref, lse_ref, cmix_ref, stream_ref, norm_ref,
):
    attended = dot(mixed_ref[0], so_ref[...]) + vec_ref[2:3]
    attended_ref[0] = attended.astype(BF)
    stream = x_ref[0].astype(F32) + mod_ref[0, 2:3] * attended
    low = stream.astype(BF)
    low_ref[0] = low
    q_ref[0] = (dot(low, xq_ref[...]) + vec_ref[3:4]).astype(BF)
    for h in range(HEADS):
        sl = slice(HD * h, HD * h + HD)
        q, k, v = q_ref[0, :, sl], k_ref[0, :, sl], v_ref[0, :, sl]
        s = dot(k, q, NT) * SCALE + mask_ref[0]
        m = jnp.max(s, axis=0, keepdims=True)
        p = jnp.exp(s - m)
        total = jnp.sum(p, axis=0, keepdims=True)
        o = dot(v, p.astype(BF), TN) * (1.0 / total)
        cmix_ref[0, :, sl] = o.T.astype(BF)
        lse_ref[0, h : h + 1, :] = m + jnp.log(total)
    stream = stream + dot(cmix_ref[0], xo_ref[...]) + vec_ref[5:6]
    stream_ref[0] = stream
    unit, _ = unit_of(stream)
    norm_ref[0] = (unit * (1.0 + mod_ref[0, 4:5]) + mod_ref[0, 3:4]).astype(BF)


def middle_forward(mixed, x, mods, vecs, second, k, v, mask, waits=()):
    n, t, d = x.shape
    tb = min(256, t)
    rows = lambda w: pl.BlockSpec((1, tb, w), lambda i, j: (i, j, 0))
    weight = lambda c: constant((d, d), (0, c))
    outs = [
        ((n, t, d), BF),
        ((n, t, d), BF),
        ((n, t, d), BF),
        ((n, HEADS, t), F32),
        ((n, t, d), BF),
        ((n, t, d), F32),
        ((n, t, d), BF),
    ]
    out_specs = [rows(d)] * 3 + [pl.BlockSpec((1, HEADS, tb), lambda i, j: (i, 0, j))] + [rows(d)] * 3
    return call(
        middle_fwd_kernel,
        (mixed, x, mods, vecs, second, second, second, k, v, mask),
        [rows(d), rows(d), whole(mods.shape), constant(vecs.shape), weight(0), weight(1), weight(2)]
        + [whole(k.shape), whole(v.shape), whole(mask.shape)],
        outs,
        out_specs,
        grid=(n, t // tb),
        waits=waits,
    )


ROOT = (2.0 / 3.141592653589793) ** 0.5


def ff_kernel(x_ref, g_ref, mod_ref, e_ref, *refs, parts):
    cs, (bias_ref, act_ref, hg_ref, fg_ref, out_ref, sum_ref, gsum_ref) = refs[:parts], refs[parts:]
    ff = bias_ref.shape[1]
    pw = ff // parts
    x = x_ref[0]
    fg = (mod_ref[0, 5:6] * g_ref[0].astype(F32)).astype(BF)
    fg_ref[0] = fg

    @pl.when(pl.program_id(1) == 0)
    def _():
        sum_ref[...] = jnp.zeros_like(sum_ref)
        gsum_ref[...] = jnp.zeros_like(gsum_ref)

    gsum_ref[0] += jnp.sum(fg.astype(F32), axis=0, keepdims=True)
    back = 0.0
    for j in range(parts):
        cols = slice(j * pw, (j + 1) * pw)
        h = dot(x, e_ref[:, cols]) + bias_ref[:, cols]
        u = dot(fg, cs[j][...], NT)
        square = h * h
        th = jnp.tanh(h * (ROOT + (ROOT * 0.044715) * square))
        half = 0.5 + 0.5 * th
        act_ref[0, :, cols] = (h * half).astype(BF)
        slope = half + h * (1.0 - th * th) * (0.5 * ROOT + (1.5 * ROOT * 0.044715) * square)
        hg = (u * slope).astype(BF)
        hg_ref[0, :, cols] = hg
        sum_ref[0, :, cols] += jnp.sum(hg.astype(F32), axis=0, keepdims=True)
        back = back + dot(hg, e_ref[:, cols], NT)
    out_ref[0] = back.astype(BF)


def feed_forward(x, g, mods, expand, contracts, bias, waits=()):
    n, t, d = x.shape
    ff, parts = bias.shape[0], len(contracts)
    tb = min(256, t)
    rows = lambda w: pl.BlockSpec((1, tb, w), lambda i, j: (i, j, 0))
    return call(
        partial(ff_kernel, parts=parts),
        (x, g, mods, expand, *[c for c, _ in contracts], bias.reshape(1, ff)),
        [rows(d), rows(d), whole(mods.shape), constant((d, ff))]
        + [constant((ff // parts, d), (0, b)) for _, b in contracts]
        + [constant((1, ff))],
        [((n, t, ff), BF)] * 2 + [((n, t, d), BF)] * 2 + [((n, 1, ff), F32), ((n, 1, d), F32)],
        [rows(ff), rows(ff), rows(d), rows(d), whole((n, 1, ff)), whole((n, 1, d))],
        grid=(n, t // tb),
        waits=waits,
        vmem=44 << 20,
    )


def fed_kernel(*refs, chunks, parts, share):
    acts, gs, cs = refs[:chunks], refs[chunks : 2 * chunks], refs[2 * chunks : 2 * chunks + parts]
    vec_ref, outs, sum_ref = refs[2 * chunks + parts], refs[2 * chunks + parts + 1 : -1], refs[-1]
    pw = cs[0].shape[0]
    total = 0.0
    for c in range(chunks):
        fed = sum(dot(acts[c][0, :, j * pw : (j + 1) * pw], cs[j][...]) for j in range(parts))
        outs[c][0] = fed.astype(BF)
        if c == 0:
            fed = fed + share * vec_ref[6:7]
        total = total + jnp.sum(gs[c][0].astype(F32) * fed, axis=0, keepdims=True)

    @pl.when(pl.program_id(1) == 0)
    def _():
        sum_ref[...] = jnp.zeros_like(sum_ref)

    sum_ref[0] += total


def fed_forward(acts, gs, contracts, vecs, d, share, waits=()):
    n, t, ff = acts[0].shape
    parts = len(contracts)
    tb = min(256, t)
    rows = lambda w: pl.BlockSpec((1, tb, w), lambda i, j: (i, j, 0))
    *feds, sums = call(
        partial(fed_kernel, chunks=len(acts), parts=parts, share=share),
        (*acts, *gs, *[c for c, _ in contracts], vecs),
        [rows(ff)] * len(acts)
        + [rows(d)] * len(acts)
        + [constant((ff // parts, d), (0, b)) for _, b in contracts]
        + [constant(vecs.shape)],
        [((n, t, d), BF)] * len(acts) + [((n, 1, d), F32)],
        [rows(d)] * len(acts) + [whole((n, 1, d))],
        grid=(n, t // tb),
        waits=waits,
        vmem=28 << 20,
    )
    return feds, sums[:, 0]


def columns_kernel(*refs, chunks):
    lefts, rights, out_ref = refs[:chunks], refs[chunks : 2 * chunks], refs[-1]
    out_ref[...] = sum(dot(a[...], b[...], TN) for a, b in zip(lefts, rights)).astype(BF)


def columns_wgrad(lefts, rights, across, width, first, into=None, waits=()):
    flat = lambda x: x.reshape(-1, x.shape[-1])
    lefts, rights = [flat(x) for x in lefts], [flat(x) for x in rights]
    d = (rights if across else lefts)[0].shape[1]
    m, wide = lefts[0].shape[1], rights[0].shape[1]
    steps = (m if across else wide) // d
    if across:
        specs = [pl.BlockSpec((x.shape[0], d), lambda s: (0, s)) for x in lefts] + [constant(x.shape) for x in rights]
    else:
        specs = [constant(x.shape) for x in lefts] + [pl.BlockSpec((x.shape[0], d), lambda s: (0, s)) for x in rights]
    ins = [*lefts, *rights]
    aliases = {}
    if into is not None:
        waits = (into, *waits)
        aliases = {len(ins): 0}
    return call(
        partial(columns_kernel, chunks=len(lefts)),
        ins,
        specs,
        [((d, width), BF)],
        [pl.BlockSpec((d, d), lambda s: (0, first + s))],
        grid=(steps,),
        waits=waits,
        vmem=44 << 20,
        aliases=aliases,
    )[0]


def finish_kernel(fed_ref, got_ref, stream_ref, mod_ref, vec_ref, out_ref):
    fed = fed_ref[0].astype(F32) + got_ref[0].astype(F32) + vec_ref[6:7]
    out_ref[0] = (stream_ref[0] + mod_ref[0, 5:6] * fed).astype(BF)


def finish_forward(fed, got, stream, mods, vecs, waits=()):
    n, t, d = stream.shape
    tb = min(256, t)
    rows = pl.BlockSpec((1, tb, d), lambda i, j: (i, j, 0))
    return call(
        finish_kernel,
        (fed, got, stream, mods, vecs),
        [rows] * 3 + [whole(mods.shape), constant(vecs.shape)],
        [((n, t, d), BF)],
        [rows],
        grid=(n, t // tb),
        waits=waits,
        vmem=16 << 20,
        token=True,
    )


def norm_back(w, unit, inverse, scale):
    u = w * (1.0 + scale)
    stream = (
        u - jnp.mean(u, axis=-1, keepdims=True) - unit * jnp.mean(u * unit, axis=-1, keepdims=True)
    ) * inverse
    return stream, jnp.sum(w, axis=0, keepdims=True), jnp.sum(w * unit, axis=0, keepdims=True)


def middle_bwd_kernel(
    pos_ref, nb_ref, got_ref, stream_ref, g_ref, mod_ref, xo_ref, xq_ref, so_ref, k_ref, v_ref, mask_ref,
    q_ref, lse_ref, attended_ref,
    cg_ref, xg_ref, ag_ref, grad_ref, sum_ref, *refs, steps,
):
    dk_ref, dv_ref, cm_ref = refs[-3:]
    refs = refs[:-3]
    tg_refs, kv_refs = refs[: len(refs) // 2], refs[len(refs) // 2 :]
    step = pl.program_id(1)
    unit, inverse = unit_of(stream_ref[0])
    w = nb_ref[0].astype(F32) + got_ref[0].astype(F32)
    back, shift, scale = norm_back(w, unit, inverse, mod_ref[0, 4:5])
    grad = back + g_ref[0].astype(F32)
    crossed = grad.astype(BF)
    cg_ref[0] = crossed
    cm_ref[...] = dot(crossed, xo_ref[...], NT).astype(BF)

    @pl.when(step == 0)
    def _():
        dk_ref[...] = jnp.zeros_like(dk_ref)
        dv_ref[...] = jnp.zeros_like(dv_ref)
        sum_ref[...] = jnp.zeros_like(sum_ref)

    for h in range(HEADS):
        sl = slice(HD * h, HD * h + HD)
        q, k, v, g = q_ref[0, :, sl], k_ref[0, :, sl], v_ref[0, :, sl], cm_ref[:, sl]
        p = jnp.exp(dot(k, q, NT) * SCALE + mask_ref[0] - lse_ref[0, h : h + 1, :])
        dp = dot(v, g, NT)
        ds = (p * (dp - jnp.sum(p * dp, axis=0, keepdims=True))).astype(BF)
        dv_ref[:, sl] += dot(p.astype(BF), g)
        dk_ref[:, sl] += dot(ds, q) * SCALE
        xg_ref[0, :, sl] = (dot(k, ds, TN) * SCALE).T.astype(BF)
    grad = grad + dot(xg_ref[0], xq_ref[...], NT)
    grad_ref[0] = grad
    attended_grad = (mod_ref[0, 2:3] * grad).astype(BF)
    ag_ref[0] = attended_grad
    tokens_grad = dot(attended_grad, so_ref[...], NT).astype(BF)
    if len(tg_refs) == 2:
        half = tokens_grad.shape[1] // 2
        low, high = tokens_grad[:, :half], tokens_grad[:, half:]
        for i in range(2):

            @pl.when(step == i)
            def _(i=i):
                tg_refs[0][0, :, i * half : (i + 1) * half] = jnp.where(pos_ref[0] == 0, low, high)
                tg_refs[1][0, :, i * half : (i + 1) * half] = jnp.where(pos_ref[0] == 0, high, low)

    else:
        tg_refs[0][0] = tokens_grad
    sums = [
        shift,
        scale,
        jnp.sum(grad * attended_ref[0].astype(F32), axis=0, keepdims=True),
        jnp.sum(crossed.astype(F32), axis=0, keepdims=True),
        jnp.sum(xg_ref[0].astype(F32), axis=0, keepdims=True),
        jnp.sum(attended_grad.astype(F32), axis=0, keepdims=True),
    ]
    for i, total in enumerate(sums):
        sum_ref[0, i : i + 1] += total

    @pl.when(step == steps - 1)
    def _():
        d = dk_ref.shape[1]
        for at, ref in ((0, dk_ref), (1, dv_ref)):
            if len(kv_refs) == 2:
                low, high = ref[:, : d // 2], ref[:, d // 2 :]
                cols = slice(at * (d // 2), (at + 1) * (d // 2))
                kv_refs[0][0, :, cols] = jnp.where(pos_ref[0] == 0, low, high).astype(BF)
                kv_refs[1][0, :, cols] = jnp.where(pos_ref[0] == 0, high, low).astype(BF)
            else:
                kv_refs[0][0, :, at * d : (at + 1) * d] = ref[...].astype(BF)


def middle_backward(pos, nb, got, stream, g, mods, second, k, v, mask, q, lse, attended, nsp, waits=()):
    n, t, d = stream.shape
    tb = min(256, t)
    rows = lambda w: pl.BlockSpec((1, tb, w), lambda i, j: (i, j, 0))
    weight = lambda c: constant((d, d), (0, c))
    stats = pl.BlockSpec((1, HEADS, tb), lambda i, j: (i, 0, j))
    pieces = 2 if nsp == 2 else 1
    kv_shape = (n, k.shape[1], 2 * d // pieces)
    tb = t // 2 if pieces == 2 else tb
    tokens = [whole((n, tb, d))] * 2 if pieces == 2 else [rows(d)]
    outs = [((n, t, d), BF)] * 3 + [((n, t, d), F32), ((n, 8, d), F32)]
    return call(
        partial(middle_bwd_kernel, steps=t // tb),
        (pos, nb, got, stream, g, mods, second, second, second, k, v, mask, q, lse, attended),
        [smem()]
        + [rows(d)] * 4
        + [whole(mods.shape), weight(2), weight(1), weight(0), whole(k.shape), whole(v.shape), whole(mask.shape)]
        + [rows(d), stats, rows(d)],
        outs + [((n, t // pieces, d), BF)] * pieces + [(kv_shape, BF)] * pieces,
        [rows(d)] * 4 + [whole((n, 8, d))] + tokens + [whole(kv_shape)] * pieces,
        grid=(n, t // tb),
        scratch=[pltpu.VMEM(k.shape[1:], F32), pltpu.VMEM(k.shape[1:], F32), pltpu.VMEM((tb, d), BF)],
        waits=waits,
        vmem=44 << 20,
    )


def self_bwd_kernel(qkv_ref, *refs, chunks, heads):
    gs, (lse_ref, grad_ref) = refs[:chunks], refs[chunks:]
    for h in range(heads):
        spans = [slice((p * heads + h) * HD, (p * heads + h + 1) * HD) for p in range(3)]
        q, k, v = [qkv_ref[0, :, sl] for sl in spans]
        g = gs[0][0, :, spans[0]]
        if chunks > 1:
            cols = [slice(i * heads * HD + h * HD, i * heads * HD + h * HD + HD) for i in range(2)]
            g = jnp.concatenate([r[0, :, c] for r in gs for c in cols], axis=0)
        p = jnp.exp(dot(k, q, NT) * SCALE - lse_ref[0, h : h + 1, :])
        dp = dot(v, g, NT)
        delta = jnp.sum(p * dp, axis=0, keepdims=True)
        ds = (p * (dp - delta)).astype(BF)
        grad_ref[0, :, spans[2]] = dot(p.astype(BF), g).astype(BF)
        grad_ref[0, :, spans[1]] = (dot(ds, q) * SCALE).astype(BF)
        grad_ref[0, :, spans[0]] = (dot(k, ds, TN) * SCALE).T.astype(BF)


def self_backward(qkv, gs, lse, waits=()):
    n, t, w = qkv.shape
    heads = w // HD // 3
    return call(
        partial(self_bwd_kernel, chunks=len(gs), heads=heads),
        (qkv, *gs, lse),
        [whole(qkv.shape)] + [whole(g.shape) for g in gs] + [whole(lse.shape)],
        [((n, t, w), BF)],
        [whole((n, t, w))],
        grid=(n,),
        waits=waits,
        vmem=60 << 20,
    )[0]


def input_bwd_kernel(*refs, chunks):
    gs, xs, w_ref = refs[:chunks], refs[chunks : 2 * chunks], refs[2 * chunks]
    outs, (sum_ref, gsum_ref) = refs[2 * chunks + 1 : -2], refs[-2:]

    @pl.when(pl.program_id(1) == 0)
    def _():
        sum_ref[...] = jnp.zeros_like(sum_ref)
        gsum_ref[...] = jnp.zeros_like(gsum_ref)

    for c in range(chunks):
        gsum_ref[0] += jnp.sum(gs[c][0].astype(F32), axis=0, keepdims=True)
        value = dot(gs[c][0], w_ref[:, : gs[c].shape[2]], NT)
        outs[c][0] = value.astype(BF)
        unit, _ = unit_of(xs[c][0].astype(F32))
        sum_ref[0, 0:1] += jnp.sum(value, axis=0, keepdims=True)
        sum_ref[0, 1:2] += jnp.sum(value * unit, axis=0, keepdims=True)


def input_backward(grad, xs, first, waits=()):
    n, t, w = grad.shape
    d = first.shape[0]
    chunks = len(xs)
    each = t // chunks
    tb = min(256, each)
    blocks = each // tb
    rows = pl.BlockSpec((1, tb, d), lambda i, j: (i, j, 0))
    return call(
        partial(input_bwd_kernel, chunks=chunks),
        (*[grad] * chunks, *xs, first),
        [pl.BlockSpec((1, tb, w), lambda i, j, c=c: (i, c * blocks + j, 0)) for c in range(chunks)]
        + [rows] * chunks
        + [constant(first.shape)],
        [((n, each, d), BF)] * chunks + [((n, 8, d), F32), ((n, 1, w), F32)],
        [rows] * chunks + [whole((n, 8, d)), whole((n, 1, w))],
        grid=(n, blocks),
        waits=waits,
        vmem=60 << 20,
    )


def last_kernel(w_ref, got_ref, x_ref, mod_ref, grad_ref, out_ref):
    unit, inverse = unit_of(x_ref[0].astype(F32))
    w = w_ref[0].astype(F32) + got_ref[0].astype(F32)
    u = w * (1.0 + mod_ref[0, 1:2])
    back = u - jnp.mean(u, axis=-1, keepdims=True) - unit * jnp.mean(u * unit, axis=-1, keepdims=True)
    out_ref[0] = grad_ref[0] + back * inverse


def last_backward(w, got, x, mods, grad, waits=()):
    n, t, d = x.shape
    tb = min(256, t)
    rows = pl.BlockSpec((1, tb, d), lambda i, j: (i, j, 0))
    return call(
        last_kernel,
        (w, got, x, mods, grad),
        [rows, rows, rows, whole(mods.shape), rows],
        [((n, t, d), F32)],
        [rows],
        grid=(n, t // tb),
        waits=waits,
        vmem=16 << 20,
        token=True,
    )


def wgrad_kernel(pos_ref, *refs, pairs, cuts, r):
    at, terms = 0, []
    for a, b in pairs:
        terms.append((refs[at : at + a], refs[at + a : at + a + b]))
        at += a + b
    outs = refs[at:]
    owns, others = outs[: len(cuts)], outs[len(cuts) :]
    first = pos_ref[1] == 0
    for (pair, a, b), own_ref, other_ref in zip(cuts, owns, others):
        left, right = terms[pair]
        value = sum(dot(x[...], y[:, a:b], TN) for x, y in zip(left, right))
        for c in range(own_ref.shape[0]):
            low, high = value[2 * c * r : 2 * c * r + r], value[2 * c * r + r : 2 * c * r + 2 * r]
            own_ref[c] = jnp.where(first, low, high).astype(BF)
            other_ref[c] = jnp.where(first, high, low).astype(BF)


def wgrad(pos, pairs, nf, waits=()):
    flat = lambda x: x.reshape(-1, x.shape[-1])
    pairs = [([flat(x) for x in a], [flat(x) for x in b]) for a, b in pairs]
    m = pairs[0][0][0].shape[1]
    r = m // nf
    cuts = []
    for i, (_, right) in enumerate(pairs):
        width = right[0].shape[1]
        cuts += [(i, a, min(a + 1152, width)) for a in range(0, width, 1152)]
    ins = [x for a, b in pairs for x in a + b]
    shapes = [((nf // 2, r, b - a), BF) for _, a, b in cuts]
    vmem = pl.BlockSpec(memory_space=pltpu.VMEM)
    outs = call(
        partial(wgrad_kernel, pairs=[(len(a), len(b)) for a, b in pairs], cuts=cuts, r=r),
        (pos, *ins),
        [smem()] + [vmem] * len(ins),
        shapes * 2,
        [vmem] * (2 * len(cuts)),
        waits=waits,
        vmem=40 << 20,
    )
    return list(outs[: len(cuts)]), list(outs[len(cuts) :])


def vectors_kernel(pos_ref, sums_ref, a_ref, gate_ref, qkv_ref, xv_ref, fed_ref, *refs, parts, r):
    hiddens, (own_ref, other_ref, all_ref) = refs[:-3], refs[-3:]
    sp = pos_ref[0]
    all_ref[...] = jnp.zeros_like(all_ref)
    sums, a_sums = jnp.sum(sums_ref[...], axis=0), jnp.sum(a_ref[...], axis=0)
    qkv = jnp.sum(qkv_ref[...], axis=0)
    own = qkv.shape[1] // 3

    def spread(row, value):
        for i in range(2):
            all_ref[row : row + 1, i * own : (i + 1) * own] = jnp.where(sp == i, value, 0.0)

    spread(0, qkv[:, :own])
    spread(1, qkv[:, 2 * own :])
    spread(4, xv_ref[...])
    fed = jnp.sum(fed_ref[...], axis=0)
    gate = jnp.sum(gate_ref[...], axis=0)
    rows = {2: sums[5:6], 3: sums[4:5], 5: sums[3:4], 6: fed, 7: a_sums[0:1], 8: a_sums[1:2]}
    rows |= {9: sums[2:3], 10: sums[0:1], 11: sums[1:2], 12: gate}
    for row, value in rows.items():
        all_ref[row : row + 1] = value
    hidden = sum(jnp.sum(h[...], axis=0) for h in hiddens)
    pw = hidden.shape[1] // parts
    for i in range(2):
        for j in range(parts):
            row = 13 + i * parts + j
            all_ref[row : row + 1] = jnp.where(sp == i, hidden[:, j * pw : (j + 1) * pw], 0.0)
    columns = all_ref[...].T
    first = pos_ref[1] == 0
    for c in range(own_ref.shape[0]):
        low, high = columns[2 * c * r : 2 * c * r + r], columns[2 * c * r + r : 2 * c * r + 2 * r]
        own_ref[c] = jnp.where(first, low, high).astype(BF)
        other_ref[c] = jnp.where(first, high, low).astype(BF)


def vector_halves(pos, sums, a_sums, gate, qkv, xv, fed, hiddens, parts, nf, waits=()):
    d = sums.shape[2]
    ins = (pos, sums, a_sums, gate, qkv, xv, fed, *hiddens)
    vmem = pl.BlockSpec(memory_space=pltpu.VMEM)
    return call(
        partial(vectors_kernel, parts=parts, r=d // nf),
        ins,
        [smem()] + [vmem] * (len(ins) - 1),
        [((nf // 2, d // nf, 128), BF)] * 2,
        [vmem] * 2,
        scratch=[pltpu.VMEM((128, d), F32)],
        waits=waits,
        vmem=16 << 20,
    )


def last_out_kernel(pos_ref, x_ref, got_ref, kv_ref, in_ref, vec_ref):
    first = pos_ref[0] == 0
    own = kv_ref.shape[1] // 4
    for p in range(5):
        x, got = x_ref[:, p * own : (p + 1) * own].astype(F32), got_ref[:, p * own : (p + 1) * own].astype(F32)
        ref, at = (kv_ref, p) if p < 2 else (in_ref, p - 2)
        ref[:, 2 * at * own : (2 * at + 1) * own] = jnp.where(first, x, got)
        ref[:, (2 * at + 1) * own : (2 * at + 2) * own] = jnp.where(first, got, x)
    vec_ref[...] = x_ref[:, 5 * own :].astype(F32) + got_ref[:, 5 * own :].astype(F32)


def last_outputs(pos, x, own):
    vmem = pl.BlockSpec(memory_space=pltpu.VMEM)
    r = x.shape[0]
    return call(
        last_out_kernel,
        (pos, x, swap(x)),
        [smem()] + [vmem] * 2,
        [((r, 4 * own), F32), ((r, 6 * own), F32), ((r, 128), F32)],
        [vmem] * 3,
        vmem=16 << 20,
    )


def ff_out_kernel(pos_ref, x_ref, got_ref, c_ref, e_ref, *, parts, nf):
    first = pos_ref[0] == 0
    r, d = x_ref.shape[0], c_ref.shape[1]
    for i in range(2):
        for j in range(parts):
            cols = slice(j * d, (j + 1) * d)
            value = jnp.where(first == (i == 0), x_ref[:, cols], got_ref[:, cols])
            c_ref[(i * parts + j) * r : (i * parts + j + 1) * r] = value.astype(F32)
    for j in range(parts):
        cols = slice((parts + j) * d, (parts + j + 1) * d)
        x, got = x_ref[:, cols].astype(F32), got_ref[:, cols].astype(F32)
        low, high = jnp.where(first, x, got), jnp.where(first, got, x)
        for f in range(nf):
            at = f * 2 * parts * r + j * r
            e_ref[:, at : at + r] = low[:, f * r : (f + 1) * r]
            e_ref[:, at + parts * r : at + parts * r + r] = high[:, f * r : (f + 1) * r]


def ff_outputs(pos, x, parts, d, nf, waits=()):
    vmem = pl.BlockSpec(memory_space=pltpu.VMEM)
    r = x.shape[0]
    return call(
        partial(ff_out_kernel, parts=parts, nf=nf),
        (pos, x, swap(x)),
        [smem()] + [vmem] * 2,
        [((2 * parts * r, d), F32), ((r, 2 * parts * d), F32)],
        [vmem] * 2,
        waits=waits,
        vmem=16 << 20,
        token=True,
    )


def core_sum_kernel(pos_ref, *refs, pieces):
    owns, gots, (y_ref, other_ref) = refs[:pieces], refs[pieces : 2 * pieces], refs[2 * pieces :]
    first = pos_ref[2] == 0
    at = 0
    for own, got in zip(owns, gots):
        cols = slice(at, at + own.shape[2])
        low = own[0].astype(F32) + got[0].astype(F32)
        high = own[1].astype(F32) + got[1].astype(F32)
        y_ref[0, :, cols] = jnp.where(first, low, high).astype(BF)
        other_ref[0, :, cols] = jnp.where(first, high, low).astype(BF)
        at += own.shape[2]


def y_sum_kernel(pos_ref, own_ref, got_ref, *outs):
    nz = len(outs)
    for d in range(nz):
        at = lax.rem(pos_ref[3] + d, nz)
        outs[d][...] = (own_ref[at].astype(F32) + got_ref[at].astype(F32)).astype(BF)


def z_sum_kernel(*refs):
    refs[-1][...] = sum(x[...].astype(F32) for x in refs[:-1]).astype(BF)


def in_vmem(kernel, ins, outs, waits=()):
    spec = pl.BlockSpec(memory_space=pltpu.VMEM)
    specs = [smem() if x.dtype == jnp.int32 else spec for x in ins]
    return call(kernel, ins, specs, [(s, BF) for s in outs], [spec] * len(outs), waits=waits, vmem=16 << 20)


def shift_z(x, nf, d):
    return lax.ppermute(x, "fsdp", [(i, (i + 4 * d) % nf) for i in range(nf)])


def cross_y(x, nf):
    return lax.ppermute(x, "fsdp", [(i, i ^ 2) for i in range(nf)])


def cross_core(x, nf):
    return lax.ppermute(x, "fsdp", [(i, i ^ 1) for i in range(nf)])


def sum_core(pos, owns, others, nf, waits=()):
    r, w = owns[0].shape[1], sum(x.shape[2] for x in owns)
    two = [pl.BlockSpec((2,) + x.shape[1:], lambda i: (i, 0, 0)) for x in owns]
    one = pl.BlockSpec((1, r, w), lambda i: (i, 0, 0))
    return call(
        partial(core_sum_kernel, pieces=len(owns)),
        (pos, *owns, *[cross_core(x, nf) for x in others]),
        [smem(), *two, *two],
        [((nf // 4, r, w), BF)] * 2,
        [one, one],
        grid=(nf // 4,),
        waits=waits,
        vmem=16 << 20,
    )


def sum_y(pos, mine, other, nf, waits=()):
    nz, r, w = mine.shape
    return in_vmem(y_sum_kernel, (pos, mine, cross_y(other, nf)), [(r, w)] * nz, waits)


def sum_z(chunks, nf, waits=()):
    got = [shift_z(chunks[d], nf, d) for d in range(1, len(chunks))]
    return in_vmem(z_sum_kernel, (chunks[0], *got), [chunks[0].shape], waits)[0]


def swap(x):
    return lax.ppermute(x, "sp", [(0, 1), (1, 0)])


def pick(x, index, axis):
    return lax.dynamic_index_in_dim(x, index, axis, keepdims=False)


def in_order(own, other, index, axis=-1):
    return jnp.where(
        index == 0, jnp.concatenate([own, other], axis=axis), jnp.concatenate([other, own], axis=axis)
    )


def halves(x, index, axis=-1):
    low, high = jnp.split(x, 2, axis=axis)
    return jnp.where(index == 0, low, high), jnp.where(index == 0, high, low)


def gather_tokens(x, nsp):
    if nsp == 2:
        return [x, swap(x)]
    return [lax.all_gather(x, "sp", axis=1, tiled=True)]


def scatter_tokens(parts, nsp):
    if nsp == 2:
        return parts[0], swap(parts[1])
    total = lax.psum_scatter(parts[0], "sp", scatter_dimension=1, tiled=True)
    return total, jnp.zeros_like(total)


def heads_to_tokens(x, nsp, index, others):
    if nsp == 2:
        half = x.shape[1] // 2
        return in_order(x[:, :half], after(swap(x[:, half:]), *others), index)
    return lax.all_to_all(x, "sp", split_axis=1, concat_axis=2, tiled=True)


def tokens_to_heads(parts, nsp):
    if nsp == 2:
        return [parts[0], swap(parts[1])]
    return [lax.all_to_all(parts[0], "sp", split_axis=2, concat_axis=1, tiled=True)]


def gather_axis(x, nsp, index, axis):
    if nsp == 2:
        return in_order(x, swap(x), index, axis)
    return lax.all_gather(x, "sp", axis=axis, tiled=True)


def scatter_axis(x, nsp, index, axis):
    if nsp == 2:
        own, other = halves(x, index, axis)
        return own.astype(F32) + swap(other.astype(BF)).astype(F32)
    return lax.psum_scatter(x.astype(BF), "sp", scatter_dimension=axis, tiled=True).astype(F32)


def sum_sp(x, nsp):
    if nsp == 2:
        return x.astype(F32) + swap(x).astype(F32)
    return lax.psum(x, "sp").astype(F32)


def gather_sp(x, nsp, index):
    if nsp == 2:
        got = swap(x)
        return [jnp.where(index == 0, x, got).astype(F32), jnp.where(index == 0, got, x).astype(F32)]
    return list(lax.all_gather(x, "sp").astype(F32))


def merge_sp(x, sums, gathers, nsp, index):
    (a, b), (c, d) = sums[0], gathers[0]
    if nsp == 2:
        got = swap(x)
        total = x[:, a:b].astype(F32) + got[:, a:b].astype(F32)
        x, got = x[:, c:d].astype(F32), got[:, c:d].astype(F32)
        return total, [jnp.where(index == 0, x, got), jnp.where(index == 0, got, x)]
    return lax.psum(x[:, a:b].astype(F32), "sp"), list(lax.all_gather(x[:, c:d], "sp").astype(F32))


def copy_kernel(at_ref, *refs, n, dim):
    ins, out, sems = refs[:n], refs[n], refs[n + 1]
    copies = []
    for i in range(n):
        index = (slice(None),) * dim + (at_ref[i],)
        copies.append(pltpu.make_async_copy(ins[i], out.at[index], sems.at[i]))
    for c in copies:
        c.start()
    for c in copies:
        c.wait()


def place_all(parts, at, dim, waits=()):
    n = len(parts)
    shape = parts[0].shape[:dim] + (n,) + parts[0].shape[dim:]
    return call(
        partial(copy_kernel, n=n, dim=dim),
        (at, *parts),
        [smem()] + anywhere(n),
        [(shape, parts[0].dtype)],
        [pl.BlockSpec(memory_space=pltpu.VMEM)],
        scratch=[pltpu.SemaphoreType.DMA((n,))],
        waits=waits,
        vmem=24 << 20,
    )[0]


def after(x, *others):
    return lax.optimization_barrier((x, *others))[0]


def column_sum(x):
    return jnp.sum(x, axis=(0, 1), dtype=F32)


def linear(x, w):
    return jnp.einsum("lsd,de->lse", x, w, preferred_element_type=F32)


def linear_back(x, w):
    return jnp.einsum("lse,de->lsd", x, w, preferred_element_type=F32)


def on_device(
    latent_tokens,
    caption_tokens,
    caption_len,
    time_embed,
    mod_table,
    self_input_weight,
    self_query_bias,
    self_value_bias,
    self_output_weight,
    self_output_bias,
    cross_query_weight,
    cross_query_bias,
    cross_keyval_weight,
    cross_value_bias,
    cross_output_weight,
    cross_output_bias,
    expand_weight,
    expand_bias,
    contract_weight,
    contract_bias,
    out_grad,
):
    nsp, nf = lax.axis_size("sp"), lax.axis_size("fsdp")
    sp, fsdp = lax.axis_index("sp"), lax.axis_index("fsdp")
    core, y, z, nz = fsdp % 2, (fsdp // 2) % 2, fsdp // 4, nf // 4
    pos = jnp.stack([sp, core, y, z]).astype(jnp.int32)
    latents, local_len, width = latent_tokens.shape
    rows = width // nf
    own = width // nsp
    hidden_rows = contract_weight.shape[0]
    hidden_own = hidden_rows // nsp
    parts = max(1, hidden_own // rows)
    block = hidden_own // parts
    part_width = nf * block

    def columns(w, pieces, groups=1):
        size = w.shape[1] // pieces // nsp // groups
        out = []
        for i in range(nsp):
            starts = [
                p * size * nsp * groups + (i * groups + g) * size for g in range(groups) for p in range(pieces)
            ]
            out.append(jnp.concatenate([w[:, a : a + size] for a in starts], axis=1))
        if nsp == 2:
            return jnp.where(sp == 0, out[0], out[1])
        return pick(jnp.stack(out), sp, 0)

    small = jnp.concatenate(
        [
            jnp.stack(
                [
                    self_query_bias,
                    self_value_bias,
                    self_output_bias,
                    cross_query_bias,
                    cross_value_bias,
                    cross_output_bias,
                    contract_bias,
                ]
            ),
            mod_table,
            expand_bias.reshape(-1, rows),
        ],
        axis=0,
    )
    smalls = small.shape[0]
    small = jnp.pad(small.T, ((0, 0), (0, 128 - smalls)))

    stream_swap = gather_tokens(latent_tokens, nsp)

    grads = gather_tokens(out_grad, nsp)
    caption_all = gather_axis(caption_tokens, nsp, sp, 1)
    stream_all = jnp.concatenate(stream_swap, axis=1)
    first = jnp.concatenate([columns(self_input_weight, 3), small], axis=1)
    second = jnp.concatenate(
        [self_output_weight, cross_query_weight, cross_output_weight, columns(cross_keyval_weight, 2)], axis=1
    )
    last = pick(expand_weight.reshape(rows, nf, nsp, parts, block), sp, 2)
    last = last.transpose(0, 2, 1, 3).reshape(rows, parts * part_width)
    contract_shard = pick(contract_weight.reshape(nsp, parts, block, width), sp, 0)
    if block == rows:
        last = jnp.concatenate([last] + [contract_shard[j] for j in range(parts)], axis=1)

    second = lax.all_gather(second, "fsdp", axis=0, tiled=True)
    ring = [first] + [shift_z(first, nf, d) for d in range(1, nz)]
    across = [cross_y(x, nf) for x in ring]
    at = jnp.stack([((z - d) % nz) * 2 + y for d in range(nz)] + [((z - d) % nz) * 2 + 1 - y for d in range(nz)])
    mine = place_all(ring + across, at.astype(jnp.int32), 0, (stream_all, last, caption_all))
    first = place_all([mine, cross_core(mine, nf)], jnp.stack([core, 1 - core]).astype(jnp.int32), 1)
    first = first.reshape(width, -1)
    whole_expand = lax.all_gather(after(last, mine), "fsdp", axis=0, tiled=True)
    if block == rows:
        whole_contracts = [(whole_expand, parts * part_width // width + j) for j in range(parts)]
    else:
        contract_shard = lax.all_gather(after(contract_shard[0], mine), "fsdp", axis=0, tiled=True)
        whole_contracts = [(contract_shard, 0)]

    smalls_all = first[:, 3 * own :].astype(F32).T

    def own_part(v):
        return pick(v.reshape(nsp, own), sp, 0)

    bias_query, bias_value = own_part(smalls_all[0]), own_part(smalls_all[1])
    bias_qkv = jnp.concatenate([bias_query, jnp.zeros_like(bias_query), bias_value]).reshape(1, 3 * own)
    vecs = smalls_all[:8]
    bias_xvalue = own_part(smalls_all[4])
    bias_expand = smalls_all[13:smalls].reshape(-1, nf, rows).transpose(1, 0, 2).reshape(nf, nsp, parts, block)
    bias_expand = pick(bias_expand, sp, 1).transpose(1, 0, 2).reshape(parts * part_width)
    mods = smalls_all[7:13][None] + time_embed.reshape(latents, 6, width)
    mods = jnp.pad(mods, ((0, 0), (0, 2), (0, 0)))

    norm_a, qkv = qkv_forward(stream_all, mods, bias_qkv, first, 3 * own)

    mixed, lse = self_forward(qkv, tuple(grads[1:]))
    second = after(second, mixed)
    whole_keyval = second[:, 3 * width :]

    keyval = linear(caption_all, whole_keyval)
    cross_keys = gather_axis(keyval[..., :own].astype(BF), nsp, sp, 2)
    cross_values = gather_axis((keyval[..., own:] + bias_xvalue).astype(BF), nsp, sp, 2)
    mixed_tokens = after(heads_to_tokens(mixed, nsp, sp, (cross_keys, cross_values)), mixed)
    place = jnp.arange(caption_all.shape[1])
    mask = jnp.where(place[None] < caption_len[:, None], 0.0, NEG).astype(F32)[..., None]
    attended, attn_low, cross_queries, cross_lse, cross_mixed, after_cross, norm_b = middle_forward(
        mixed_tokens, latent_tokens, mods, vecs, second, cross_keys, cross_values, mask
    )

    norm_bs = gather_tokens(norm_b, nsp)
    ff_out = [None] * len(norm_bs)
    waits = ()
    for c in reversed(range(len(norm_bs))):
        ff_out[c] = feed_forward(norm_bs[c], grads[c], mods, whole_expand, whole_contracts, bias_expand, waits)
        waits = (ff_out[c][3],)
    acts, hidden_grads, fed_grads, norm_b_grads, hidden_sums, fed_sums = zip(*ff_out)
    norm_b_terms = scatter_tokens(norm_b_grads, nsp)
    expand_bgrad = sum(jnp.sum(x, axis=(0, 1)) for x in hidden_sums)
    if nsp == 2:
        contract_bgrad = jnp.sum(fed_sums[0], axis=(0, 1))
    else:
        contract_bgrad = column_sum(mods[:, 5:6] * out_grad.astype(F32))
    if block == rows:
        ff_own = columns_wgrad(acts, fed_grads, True, 2 * parts * width, 0)
        ff_own = columns_wgrad(norm_bs, hidden_grads, False, 2 * parts * width, parts, ff_own, (norm_b_terms[1],))
        ff_done = ff_own
        ff_own = lax.psum_scatter(ff_own, "fsdp", scatter_dimension=0, tiled=True)
        ff_sp = gather_sp(ff_own, nsp, sp)
        contract_sp, expand_sp = [g[:, : parts * width] for g in ff_sp], [g[:, parts * width :] for g in ff_sp]
    else:
        contract_own = jnp.einsum("lsd,lse->de", acts[0], fed_grads[0], preferred_element_type=F32).astype(BF)
        expand_own = jnp.einsum("lsd,lse->de", norm_bs[0], hidden_grads[0], preferred_element_type=F32).astype(BF)
        ff_done = expand_own
        contract_sp = gather_sp(lax.psum_scatter(contract_own, "fsdp", scatter_dimension=0, tiled=True), nsp, sp)
        expand_sp = gather_sp(lax.psum_scatter(expand_own, "fsdp", scatter_dimension=0, tiled=True), nsp, sp)

    crossed_grad, xquery_grad, attended_grad, attn_stream_grad, sums, *rest = middle_backward(
        pos, *norm_b_terms, after_cross, out_grad, mods, second, cross_keys, cross_values, mask,
        cross_queries, cross_lse, attended, nsp, waits=(ff_done,),
    )
    shift_b_grad, scale_b_grad, gate_a_grad = sums[:, 0], sums[:, 1], sums[:, 2]
    tokens_grads, keyval_parts = rest[: len(rest) // 2], rest[len(rest) // 2 :]
    mixed_grads = tokens_to_heads(tokens_grads, nsp)
    feds, gate_b_grad = fed_forward(
        acts, grads, whole_contracts, vecs, width, 1.0 if nsp == 2 else 1.0 / nsp, (attended_grad,)
    )
    fed_terms = scatter_tokens(feds, nsp)
    if nsp == 2:
        keyval_grad = (keyval_parts[0].astype(F32) + swap(keyval_parts[1]).astype(F32)).astype(BF)
    else:
        dk, dv = jnp.split(keyval_parts[0], 2, axis=-1)
        keyval_grad = jnp.concatenate([scatter_axis(dk, nsp, sp, 2), scatter_axis(dv, nsp, sp, 2)], axis=-1)
        keyval_grad = keyval_grad.astype(BF)
    outer_halves = wgrad(
        pos,
        [([attn_low], [xquery_grad]), ([cross_mixed], [crossed_grad]), ([mixed_tokens], [attended_grad])],
        nf,
        (feds[0], mixed_grads[-1], keyval_grad),
    )
    outer_core = sum_core(pos, *outer_halves, nf)
    caption_grad = scatter_axis(linear_back(keyval_grad, whole_keyval), nsp, sp, 1)
    xvalue_bgrad = column_sum(keyval_grad[..., own:])

    projected_grad = self_backward(qkv, mixed_grads, lse, (outer_core[0],))
    input_out = input_backward(projected_grad, stream_swap, first)
    norm_a_terms = scatter_tokens(list(input_out[:-2]), nsp)
    shift_a_grad, scale_a_grad = input_out[-2][:, 0], input_out[-2][:, 1]
    if nsp == 2 and block == rows:
        vector_parts = vector_halves(
            pos, sums, input_out[-2], gate_b_grad[:, None], input_out[-1], xvalue_bgrad[None], fed_sums[0],
            hidden_sums, parts, nf,
        )
    else:

        def spread(x):
            return jnp.where(jnp.arange(nsp)[:, None] == sp, x[None], 0.0).reshape(nsp * x.shape[0])

        qkv_bgrad = column_sum(input_out[-1])
        expand_bias_part = jnp.where(
            jnp.arange(nsp)[None, :, None, None] == sp,
            expand_bgrad.reshape(parts, nf, block).transpose(1, 0, 2)[:, None],
            0.0,
        ).reshape(nf, -1, rows)
        vectors = jnp.stack(
            [
                spread(qkv_bgrad[:own]),
                spread(qkv_bgrad[2 * own :]),
                jnp.sum(sums[:, 5], axis=0),
                jnp.sum(sums[:, 4], axis=0),
                spread(xvalue_bgrad),
                jnp.sum(sums[:, 3], axis=0),
                contract_bgrad,
                jnp.sum(shift_a_grad, axis=0),
                jnp.sum(scale_a_grad, axis=0),
                jnp.sum(gate_a_grad, axis=0),
                jnp.sum(shift_b_grad, axis=0),
                jnp.sum(scale_b_grad, axis=0),
                jnp.sum(gate_b_grad, axis=0),
            ]
        )
        vectors = jnp.concatenate([vectors, expand_bias_part.transpose(1, 0, 2).reshape(-1, width)])
        vectors = jnp.pad(vectors.T, ((0, 0), (0, 128 - vectors.shape[0]))).astype(BF)
        vectors = vectors.reshape(nf // 2, 2, rows, 128)
        vector_parts = (pick(vectors, core, 1), pick(vectors, 1 - core, 1))
    count = 13 + hidden_rows // rows
    input_own, input_other = wgrad(
        pos, [([caption_all], [keyval_grad]), ([norm_a], [projected_grad])], nf, (vector_parts[0], fed_terms[1])
    )
    outer_y = sum_y(pos, *outer_core, nf, waits=(input_own[0],))
    input_core = sum_core(
        pos, input_own + [vector_parts[0]], input_other + [vector_parts[1]], nf, waits=(outer_y[0],)
    )
    outer_own = sum_z(outer_y, nf, waits=(input_core[0], norm_a_terms[1]))
    input_y = sum_y(pos, *input_core, nf, waits=(outer_own,))
    latent_grad, *tokens = last_backward(*norm_a_terms, latent_tokens, mods, attn_stream_grad, (input_y[0],))
    block_out, token = finish_forward(*fed_terms, after_cross, mods, vecs, waits=(input_y[0],))
    tokens.append(token)

    if nsp == 2 and block == rows:
        contract_out, expand_out, token = ff_outputs(pos, ff_own, parts, width, nf, (input_y[0],))
        tokens.append(token)
    else:
        contract_out = jnp.concatenate(
            [
                g[:, j * width : (j + 1) * width]
                for g in contract_sp
                for j in range(contract_sp[0].shape[1] // width)
            ],
            axis=0,
        )
        expand_out = jnp.stack(
            [g.reshape(rows, parts, nf, block).transpose(0, 2, 1, 3) for g in expand_sp], axis=2
        ).reshape(rows, -1)
    embed_part = jnp.stack(
        [shift_a_grad, scale_a_grad, gate_a_grad, shift_b_grad, scale_b_grad, gate_b_grad], axis=1
    )
    time_grad = sum_sp(embed_part.reshape(latents, 6 * width), nsp)
    outer_sum = sum_sp(outer_own, nsp)
    xquery_out, xoutput_out, output_out = [outer_sum[:, i * width : (i + 1) * width] for i in range(3)]
    input_own = sum_z(input_y, nf, waits=(*tokens, time_grad))
    if nsp == 2:
        keyval_out, input_wout, owned = last_outputs(pos, input_own, own)
    else:
        inputs = list(lax.all_gather(input_own[:, : 5 * own], "sp").astype(F32))
        keyval_out = jnp.concatenate([g[:, p * own : (p + 1) * own] for p in range(2) for g in inputs], axis=1)
        input_wout = jnp.concatenate([g[:, p * own : (p + 1) * own] for p in range(2, 5) for g in inputs], axis=1)
        owned = sum_sp(input_own[:, 5 * own :], nsp)
    owned = owned[:, :count].T
    expand_bout = owned[13:count].reshape(hidden_rows)

    table_out = owned[7:13]
    return (
        block_out,
        latent_grad,
        caption_grad,
        time_grad,
        table_out,
        input_wout,
        owned[0],
        owned[1],
        output_out,
        owned[2],
        xquery_out,
        owned[3],
        keyval_out,
        owned[4],
        xoutput_out,
        owned[5],
        expand_out,
        expand_bout,
        contract_out,
        owned[6],
    )


def solution(mesh):
    row, vec, tokens = P("fsdp", None), P("fsdp"), P("fsdp", "sp", None)
    in_specs = (
        (tokens, tokens, vec, row, P(None, "fsdp"), row, vec, vec)
        + (row, vec) * 2
        + (row, vec) * 4
        + (tokens,)
    )
    out_specs = (
        (tokens, tokens, tokens, row, P(None, "fsdp"), row, vec, vec) + (row, vec) * 2 + (row, vec) * 4
    )
    return jax.shard_map(
        on_device, mesh=mesh, in_specs=in_specs, out_specs=out_specs, check_vma=False
    )
```

```python
from functools import partial

import jax
import jax.numpy as jnp
from jax import lax
from jax.experimental import pallas as pl
from jax.experimental.pallas import tpu as pltpu
from jax.sharding import PartitionSpec as P

HEADS = 16
HD = 72
GROUPS = 2
SCALE = HD**-0.5
COST = 1 << 20
EPS = 1e-06
NEG = -1e30
F32 = jnp.float32
BF = jnp.bfloat16
NT = (((1,), (1,)), ((), ()))
TN = (((0,), (0,)), ((), ()))
NN = (((1,), (0,)), ((), ()))
VMEM = 56 << 20


def dot(a, b, dims=NN):
    return lax.dot_general(a, b, dims, preferred_element_type=F32)


def whole(shape, n=1):
    return pl.BlockSpec((1,) + tuple(shape[1:]), lambda i, *_: (i,) + (0,) * (len(shape) - 1))


def constant(shape, at=None):
    at = at or (0,) * len(shape)
    return pl.BlockSpec(tuple(shape), lambda *_: at, pipeline_mode=pl.Buffered(1))


def anywhere(n):
    return [pl.BlockSpec(memory_space=pl.ANY)] * n


def smem():
    return pl.BlockSpec(memory_space=pltpu.SMEM)


def call(kernel, ins, in_specs, outs, out_specs, grid=(), scratch=(), waits=(), vmem=VMEM, aliases=None, token=False):
    n_in, n_wait = len(ins), len(waits)
    if token:
        outs, out_specs = [*outs, ((8, 128), F32)], [*out_specs, pl.BlockSpec((8, 128), lambda *_: (0, 0))]

    def body(*refs):
        if token:
            at = n_in + n_wait + len(outs) - 1
            refs[at][...] = jnp.zeros((8, 128), F32)
            refs = refs[:at] + refs[at + 1 :]
        kernel(*refs[:n_in], *refs[n_in + n_wait :])

    return pl.pallas_call(
        body,
        name=(kernel.func if isinstance(kernel, partial) else kernel).__name__,
        grid=grid,
        in_specs=list(in_specs) + anywhere(n_wait),
        out_specs=out_specs,
        out_shape=[jax.ShapeDtypeStruct(s, d) for s, d in outs],
        scratch_shapes=list(scratch),
        input_output_aliases=aliases or {},
        compiler_params=pltpu.CompilerParams(vmem_limit_bytes=vmem),
        cost_estimate=pl.CostEstimate(flops=0, bytes_accessed=COST, transcendentals=0),
    )(*ins, *waits)


def unit_of(v):
    centre = v - jnp.mean(v, axis=-1, keepdims=True)
    inverse = lax.rsqrt(jnp.mean(centre * centre, axis=-1, keepdims=True) + EPS)
    return centre * inverse, inverse


def qkv_kernel(x_ref, mod_ref, bias_ref, w_ref, norm_ref, qkv_ref):
    unit, _ = unit_of(x_ref[0].astype(F32))
    norm = (unit * (1.0 + mod_ref[0, 1:2]) + mod_ref[0, 0:1]).astype(BF)
    norm_ref[0] = norm
    qkv_ref[0] = (dot(norm, w_ref[:, : bias_ref.shape[1]]) + bias_ref[...]).astype(BF)


def qkv_forward(x, mods, bias, first, width3, waits=()):
    n, t, d = x.shape
    tb = min(256, t)
    rows = lambda w: pl.BlockSpec((1, tb, w), lambda i, j: (i, j, 0))
    return call(
        qkv_kernel,
        (x, mods, bias, first),
        [rows(d), whole(mods.shape), constant(bias.shape), constant(first.shape)],
        [((n, t, d), BF), ((n, t, width3), BF)],
        [rows(d), rows(width3)],
        grid=(n, t // tb),
        waits=waits,
    )


def self_fwd_kernel(qkv_ref, *refs, heads):
    o_ref, lse_ref = refs[-2:]
    for h in range(heads):
        q, k, v = [qkv_ref[0, :, (p * heads + h) * HD : (p * heads + h + 1) * HD] for p in range(3)]
        s = dot(k, q, NT) * SCALE
        m = jnp.max(s, axis=0, keepdims=True)
        p = jnp.exp(s - m)
        total = jnp.sum(p, axis=0, keepdims=True)
        o = dot(v, p.astype(BF), TN) * (1.0 / total)
        o_ref[0, :, h * HD : h * HD + HD] = o.T.astype(BF)
        lse_ref[0, h : h + 1, :] = m + jnp.log(total)


def self_forward(qkv, waits=()):
    n, t, w = qkv.shape
    heads = w // HD // 3
    outs = [((n, t, w // 3), BF), ((n, heads, t), F32)]
    return call(
        partial(self_fwd_kernel, heads=heads),
        (qkv,),
        [whole(qkv.shape)],
        outs,
        [whole(s) for s, _ in outs],
        grid=(n,),
        waits=waits,
        vmem=40 << 20,
    )


def middle_fwd_kernel(
    mixed_ref, x_ref, mod_ref, vec_ref, so_ref, xq_ref, xo_ref, k_ref, v_ref, mask_ref,
    attended_ref, low_ref, q_ref, lse_ref, cmix_ref, stream_ref, norm_ref,
):
    attended = dot(mixed_ref[0], so_ref[...]) + vec_ref[2:3]
    attended_ref[0] = attended.astype(BF)
    stream = x_ref[0].astype(F32) + mod_ref[0, 2:3] * attended
    low = stream.astype(BF)
    low_ref[0] = low
    q_ref[0] = (dot(low, xq_ref[...]) + vec_ref[3:4]).astype(BF)
    for h in range(HEADS):
        sl = slice(HD * h, HD * h + HD)
        q, k, v = q_ref[0, :, sl], k_ref[0, :, sl], v_ref[0, :, sl]
        s = dot(k, q, NT) * SCALE + mask_ref[0]
        m = jnp.max(s, axis=0, keepdims=True)
        p = jnp.exp(s - m)
        total = jnp.sum(p, axis=0, keepdims=True)
        o = dot(v, p.astype(BF), TN) * (1.0 / total)
        cmix_ref[0, :, sl] = o.T.astype(BF)
        lse_ref[0, h : h + 1, :] = m + jnp.log(total)
    stream = stream + dot(cmix_ref[0], xo_ref[...]) + vec_ref[5:6]
    stream_ref[0] = stream
    unit, _ = unit_of(stream)
    norm_ref[0] = (unit * (1.0 + mod_ref[0, 4:5]) + mod_ref[0, 3:4]).astype(BF)


def middle_forward(mixed, x, mods, vecs, second, k, v, mask, waits=()):
    n, t, d = x.shape
    tb = min(256, t)
    rows = lambda w: pl.BlockSpec((1, tb, w), lambda i, j: (i, j, 0))
    weight = lambda c: constant((d, d), (0, c))
    outs = [
        ((n, t, d), BF),
        ((n, t, d), BF),
        ((n, t, d), BF),
        ((n, HEADS, t), F32),
        ((n, t, d), BF),
        ((n, t, d), F32),
        ((n, t, d), BF),
    ]
    out_specs = [rows(d)] * 3 + [pl.BlockSpec((1, HEADS, tb), lambda i, j: (i, 0, j))] + [rows(d)] * 3
    return call(
        middle_fwd_kernel,
        (mixed, x, mods, vecs, second, second, second, k, v, mask),
        [rows(d), rows(d), whole(mods.shape), constant(vecs.shape), weight(0), weight(1), weight(2)]
        + [whole(k.shape), whole(v.shape), whole(mask.shape)],
        outs,
        out_specs,
        grid=(n, t // tb),
        waits=waits,
    )


ROOT = (2.0 / 3.141592653589793) ** 0.5


def ff_kernel(x_ref, g_ref, mod_ref, e_ref, *refs, parts):
    cs, (bias_ref, act_ref, hg_ref, fg_ref, out_ref, sum_ref, gsum_ref) = refs[:parts], refs[parts:]
    ff = bias_ref.shape[1]
    pw = ff // parts
    x = x_ref[0]
    fg = (mod_ref[0, 5:6] * g_ref[0].astype(F32)).astype(BF)
    fg_ref[0] = fg

    @pl.when(pl.program_id(1) == 0)
    def _():
        sum_ref[...] = jnp.zeros_like(sum_ref)
        gsum_ref[...] = jnp.zeros_like(gsum_ref)

    gsum_ref[0] += jnp.sum(fg.astype(F32), axis=0, keepdims=True)
    back = 0.0
    for j in range(parts):
        cols = slice(j * pw, (j + 1) * pw)
        h = dot(x, e_ref[:, cols]) + bias_ref[:, cols]
        u = dot(fg, cs[j][...], NT)
        square = h * h
        th = jnp.tanh(h * (ROOT + (ROOT * 0.044715) * square))
        half = 0.5 + 0.5 * th
        act_ref[0, :, cols] = (h * half).astype(BF)
        slope = half + h * (1.0 - th * th) * (0.5 * ROOT + (1.5 * ROOT * 0.044715) * square)
        hg = (u * slope).astype(BF)
        hg_ref[0, :, cols] = hg
        sum_ref[0, :, cols] += jnp.sum(hg.astype(F32), axis=0, keepdims=True)
        back = back + dot(hg, e_ref[:, cols], NT)
    out_ref[0] = back.astype(BF)


def feed_forward(x, g, mods, expand, contracts, bias, waits=()):
    n, t, d = x.shape
    ff, parts = bias.shape[0], len(contracts)
    tb = min(256, t)
    rows = lambda w: pl.BlockSpec((1, tb, w), lambda i, j: (i, j, 0))
    return call(
        partial(ff_kernel, parts=parts),
        (x, g, mods, expand, *[c for c, _ in contracts], bias.reshape(1, ff)),
        [rows(d), rows(d), whole(mods.shape), constant((d, ff))]
        + [constant((ff // parts, d), (0, b)) for _, b in contracts]
        + [constant((1, ff))],
        [((n, t, ff), BF)] * 2 + [((n, t, d), BF)] * 2 + [((n, 1, ff), F32), ((n, 1, d), F32)],
        [rows(ff), rows(ff), rows(d), rows(d), whole((n, 1, ff)), whole((n, 1, d))],
        grid=(n, t // tb),
        waits=waits,
        vmem=44 << 20,
    )


def fed_kernel(*refs, chunks, parts, share):
    acts, gs, cs = refs[:chunks], refs[chunks : 2 * chunks], refs[2 * chunks : 2 * chunks + parts]
    vec_ref, outs, sum_ref = refs[2 * chunks + parts], refs[2 * chunks + parts + 1 : -1], refs[-1]
    pw = cs[0].shape[0]
    total = 0.0
    for c in range(chunks):
        fed = sum(dot(acts[c][0, :, j * pw : (j + 1) * pw], cs[j][...]) for j in range(parts))
        outs[c][0] = fed.astype(BF)
        if c == 0:
            fed = fed + share * vec_ref[6:7]
        total = total + jnp.sum(gs[c][0].astype(F32) * fed, axis=0, keepdims=True)

    @pl.when(pl.program_id(1) == 0)
    def _():
        sum_ref[...] = jnp.zeros_like(sum_ref)

    sum_ref[0] += total


def fed_forward(acts, gs, contracts, vecs, d, share, waits=()):
    n, t, ff = acts[0].shape
    parts = len(contracts)
    tb = min(256, t)
    rows = lambda w: pl.BlockSpec((1, tb, w), lambda i, j: (i, j, 0))
    *feds, sums = call(
        partial(fed_kernel, chunks=len(acts), parts=parts, share=share),
        (*acts, *gs, *[c for c, _ in contracts], vecs),
        [rows(ff)] * len(acts)
        + [rows(d)] * len(acts)
        + [constant((ff // parts, d), (0, b)) for _, b in contracts]
        + [constant(vecs.shape)],
        [((n, t, d), BF)] * len(acts) + [((n, 1, d), F32)],
        [rows(d)] * len(acts) + [whole((n, 1, d))],
        grid=(n, t // tb),
        waits=waits,
        vmem=28 << 20,
    )
    return feds, sums[:, 0]


def columns_kernel(*refs, chunks):
    lefts, rights, out_ref = refs[:chunks], refs[chunks : 2 * chunks], refs[-1]
    out_ref[...] = sum(dot(a[...], b[...], TN) for a, b in zip(lefts, rights)).astype(BF)


def columns_wgrad(lefts, rights, across, width, first, into=None, waits=()):
    flat = lambda x: x.reshape(-1, x.shape[-1])
    lefts, rights = [flat(x) for x in lefts], [flat(x) for x in rights]
    d = (rights if across else lefts)[0].shape[1]
    m, wide = lefts[0].shape[1], rights[0].shape[1]
    steps = (m if across else wide) // d
    if across:
        specs = [pl.BlockSpec((x.shape[0], d), lambda s: (0, s)) for x in lefts] + [constant(x.shape) for x in rights]
    else:
        specs = [constant(x.shape) for x in lefts] + [pl.BlockSpec((x.shape[0], d), lambda s: (0, s)) for x in rights]
    ins = [*lefts, *rights]
    aliases = {}
    if into is not None:
        waits = (into, *waits)
        aliases = {len(ins): 0}
    return call(
        partial(columns_kernel, chunks=len(lefts)),
        ins,
        specs,
        [((d, width), BF)],
        [pl.BlockSpec((d, d), lambda s: (0, first + s))],
        grid=(steps,),
        waits=waits,
        vmem=44 << 20,
        aliases=aliases,
    )[0]


def finish_kernel(fed_ref, got_ref, stream_ref, mod_ref, vec_ref, out_ref):
    fed = fed_ref[0].astype(F32) + got_ref[0].astype(F32) + vec_ref[6:7]
    out_ref[0] = (stream_ref[0] + mod_ref[0, 5:6] * fed).astype(BF)


def finish_forward(fed, got, stream, mods, vecs, waits=()):
    n, t, d = stream.shape
    tb = min(256, t)
    rows = pl.BlockSpec((1, tb, d), lambda i, j: (i, j, 0))
    return call(
        finish_kernel,
        (fed, got, stream, mods, vecs),
        [rows] * 3 + [whole(mods.shape), constant(vecs.shape)],
        [((n, t, d), BF)],
        [rows],
        grid=(n, t // tb),
        waits=waits,
        vmem=16 << 20,
        token=True,
    )


def norm_back(w, unit, inverse, scale):
    u = w * (1.0 + scale)
    stream = (
        u - jnp.mean(u, axis=-1, keepdims=True) - unit * jnp.mean(u * unit, axis=-1, keepdims=True)
    ) * inverse
    return stream, jnp.sum(w, axis=0, keepdims=True), jnp.sum(w * unit, axis=0, keepdims=True)


def middle_bwd_kernel(
    pos_ref, nb_ref, got_ref, stream_ref, g_ref, mod_ref, xo_ref, xq_ref, so_ref, k_ref, v_ref, mask_ref,
    q_ref, lse_ref, attended_ref,
    cg_ref, xg_ref, ag_ref, grad_ref, sum_ref, *refs, steps,
):
    dk_ref, dv_ref, cm_ref = refs[-3:]
    refs = refs[:-3]
    tg_refs, kv_refs = refs[: len(refs) // 2], refs[len(refs) // 2 :]
    step = pl.program_id(1)
    unit, inverse = unit_of(stream_ref[0])
    w = nb_ref[0].astype(F32) + got_ref[0].astype(F32)
    back, shift, scale = norm_back(w, unit, inverse, mod_ref[0, 4:5])
    grad = back + g_ref[0].astype(F32)
    crossed = grad.astype(BF)
    cg_ref[0] = crossed
    cm_ref[...] = dot(crossed, xo_ref[...], NT).astype(BF)

    @pl.when(step == 0)
    def _():
        dk_ref[...] = jnp.zeros_like(dk_ref)
        dv_ref[...] = jnp.zeros_like(dv_ref)
        sum_ref[...] = jnp.zeros_like(sum_ref)

    for h in range(HEADS):
        sl = slice(HD * h, HD * h + HD)
        q, k, v, g = q_ref[0, :, sl], k_ref[0, :, sl], v_ref[0, :, sl], cm_ref[:, sl]
        p = jnp.exp(dot(k, q, NT) * SCALE + mask_ref[0] - lse_ref[0, h : h + 1, :])
        dp = dot(v, g, NT)
        ds = (p * (dp - jnp.sum(p * dp, axis=0, keepdims=True))).astype(BF)
        dv_ref[:, sl] += dot(p.astype(BF), g)
        dk_ref[:, sl] += dot(ds, q) * SCALE
        xg_ref[0, :, sl] = (dot(k, ds, TN) * SCALE).T.astype(BF)
    grad = grad + dot(xg_ref[0], xq_ref[...], NT)
    grad_ref[0] = grad
    attended_grad = (mod_ref[0, 2:3] * grad).astype(BF)
    ag_ref[0] = attended_grad
    tokens_grad = dot(attended_grad, so_ref[...], NT).astype(BF)
    if len(tg_refs) == 2:
        half = tokens_grad.shape[1] // 2
        low, high = tokens_grad[:, :half], tokens_grad[:, half:]
        for i in range(2):

            @pl.when(step == i)
            def _(i=i):
                tg_refs[0][0, :, i * half : (i + 1) * half] = jnp.where(pos_ref[0] == 0, low, high)
                tg_refs[1][0, :, i * half : (i + 1) * half] = jnp.where(pos_ref[0] == 0, high, low)

    else:
        tg_refs[0][0] = tokens_grad
    sums = [
        shift,
        scale,
        jnp.sum(grad * attended_ref[0].astype(F32), axis=0, keepdims=True),
        jnp.sum(crossed.astype(F32), axis=0, keepdims=True),
        jnp.sum(xg_ref[0].astype(F32), axis=0, keepdims=True),
        jnp.sum(attended_grad.astype(F32), axis=0, keepdims=True),
    ]
    for i, total in enumerate(sums):
        sum_ref[0, i : i + 1] += total

    @pl.when(step == steps - 1)
    def _():
        d = dk_ref.shape[1]
        for at, ref in ((0, dk_ref), (1, dv_ref)):
            if len(kv_refs) == 2:
                low, high = ref[:, : d // 2], ref[:, d // 2 :]
                cols = slice(at * (d // 2), (at + 1) * (d // 2))
                kv_refs[0][0, :, cols] = jnp.where(pos_ref[0] == 0, low, high).astype(BF)
                kv_refs[1][0, :, cols] = jnp.where(pos_ref[0] == 0, high, low).astype(BF)
            else:
                kv_refs[0][0, :, at * d : (at + 1) * d] = ref[...].astype(BF)


def middle_backward(pos, nb, got, stream, g, mods, second, k, v, mask, q, lse, attended, nsp, waits=()):
    n, t, d = stream.shape
    tb = min(256, t)
    rows = lambda w: pl.BlockSpec((1, tb, w), lambda i, j: (i, j, 0))
    weight = lambda c: constant((d, d), (0, c))
    stats = pl.BlockSpec((1, HEADS, tb), lambda i, j: (i, 0, j))
    pieces = 2 if nsp == 2 else 1
    kv_shape = (n, k.shape[1], 2 * d // pieces)
    tb = t // 2 if pieces == 2 else tb
    tokens = [whole((n, tb, d))] * 2 if pieces == 2 else [rows(d)]
    outs = [((n, t, d), BF)] * 3 + [((n, t, d), F32), ((n, 8, d), F32)]
    return call(
        partial(middle_bwd_kernel, steps=t // tb),
        (pos, nb, got, stream, g, mods, second, second, second, k, v, mask, q, lse, attended),
        [smem()]
        + [rows(d)] * 4
        + [whole(mods.shape), weight(2), weight(1), weight(0), whole(k.shape), whole(v.shape), whole(mask.shape)]
        + [rows(d), stats, rows(d)],
        outs + [((n, t // pieces, d), BF)] * pieces + [(kv_shape, BF)] * pieces,
        [rows(d)] * 4 + [whole((n, 8, d))] + tokens + [whole(kv_shape)] * pieces,
        grid=(n, t // tb),
        scratch=[pltpu.VMEM(k.shape[1:], F32), pltpu.VMEM(k.shape[1:], F32), pltpu.VMEM((tb, d), BF)],
        waits=waits,
        vmem=44 << 20,
    )


def self_bwd_kernel(qkv_ref, *refs, chunks, heads):
    gs, (lse_ref, grad_ref) = refs[:chunks], refs[chunks:]
    for h in range(heads):
        spans = [slice((p * heads + h) * HD, (p * heads + h + 1) * HD) for p in range(3)]
        q, k, v = [qkv_ref[0, :, sl] for sl in spans]
        g = gs[0][0, :, spans[0]]
        if chunks > 1:
            cols = [slice(i * heads * HD + h * HD, i * heads * HD + h * HD + HD) for i in range(2)]
            g = jnp.concatenate([r[0, :, c] for r in gs for c in cols], axis=0)
        p = jnp.exp(dot(k, q, NT) * SCALE - lse_ref[0, h : h + 1, :])
        dp = dot(v, g, NT)
        delta = jnp.sum(p * dp, axis=0, keepdims=True)
        ds = (p * (dp - delta)).astype(BF)
        grad_ref[0, :, spans[2]] = dot(p.astype(BF), g).astype(BF)
        grad_ref[0, :, spans[1]] = (dot(ds, q) * SCALE).astype(BF)
        grad_ref[0, :, spans[0]] = (dot(k, ds, TN) * SCALE).T.astype(BF)


def self_backward(qkv, gs, lse, waits=()):
    n, t, w = qkv.shape
    heads = w // HD // 3
    return call(
        partial(self_bwd_kernel, chunks=len(gs), heads=heads),
        (qkv, *gs, lse),
        [whole(qkv.shape)] + [whole(g.shape) for g in gs] + [whole(lse.shape)],
        [((n, t, w), BF)],
        [whole((n, t, w))],
        grid=(n,),
        waits=waits,
        vmem=60 << 20,
    )[0]


def input_bwd_kernel(*refs, chunks):
    gs, xs, w_ref = refs[:chunks], refs[chunks : 2 * chunks], refs[2 * chunks]
    outs, (sum_ref, gsum_ref) = refs[2 * chunks + 1 : -2], refs[-2:]

    @pl.when(pl.program_id(1) == 0)
    def _():
        sum_ref[...] = jnp.zeros_like(sum_ref)
        gsum_ref[...] = jnp.zeros_like(gsum_ref)

    for c in range(chunks):
        gsum_ref[0] += jnp.sum(gs[c][0].astype(F32), axis=0, keepdims=True)
        value = dot(gs[c][0], w_ref[:, : gs[c].shape[2]], NT)
        outs[c][0] = value.astype(BF)
        unit, _ = unit_of(xs[c][0].astype(F32))
        sum_ref[0, 0:1] += jnp.sum(value, axis=0, keepdims=True)
        sum_ref[0, 1:2] += jnp.sum(value * unit, axis=0, keepdims=True)


def input_backward(grad, xs, first, waits=()):
    n, t, w = grad.shape
    d = first.shape[0]
    chunks = len(xs)
    each = t // chunks
    tb = min(256, each)
    blocks = each // tb
    rows = pl.BlockSpec((1, tb, d), lambda i, j: (i, j, 0))
    return call(
        partial(input_bwd_kernel, chunks=chunks),
        (*[grad] * chunks, *xs, first),
        [pl.BlockSpec((1, tb, w), lambda i, j, c=c: (i, c * blocks + j, 0)) for c in range(chunks)]
        + [rows] * chunks
        + [constant(first.shape)],
        [((n, each, d), BF)] * chunks + [((n, 8, d), F32), ((n, 1, w), F32)],
        [rows] * chunks + [whole((n, 8, d)), whole((n, 1, w))],
        grid=(n, blocks),
        waits=waits,
        vmem=60 << 20,
    )


def last_kernel(w_ref, got_ref, x_ref, mod_ref, grad_ref, out_ref):
    unit, inverse = unit_of(x_ref[0].astype(F32))
    w = w_ref[0].astype(F32) + got_ref[0].astype(F32)
    u = w * (1.0 + mod_ref[0, 1:2])
    back = u - jnp.mean(u, axis=-1, keepdims=True) - unit * jnp.mean(u * unit, axis=-1, keepdims=True)
    out_ref[0] = grad_ref[0] + back * inverse


def last_backward(w, got, x, mods, grad, waits=()):
    n, t, d = x.shape
    tb = min(256, t)
    rows = pl.BlockSpec((1, tb, d), lambda i, j: (i, j, 0))
    return call(
        last_kernel,
        (w, got, x, mods, grad),
        [rows, rows, rows, whole(mods.shape), rows],
        [((n, t, d), F32)],
        [rows],
        grid=(n, t // tb),
        waits=waits,
        vmem=16 << 20,
        token=True,
    )


def wgrad_kernel(pos_ref, *refs, pairs, cuts, r):
    at, terms = 0, []
    for a, b in pairs:
        terms.append((refs[at : at + a], refs[at + a : at + a + b]))
        at += a + b
    outs = refs[at:]
    owns, others = outs[: len(cuts)], outs[len(cuts) :]
    first = pos_ref[1] == 0
    for (pair, a, b), own_ref, other_ref in zip(cuts, owns, others):
        left, right = terms[pair]
        value = sum(dot(x[...], y[:, a:b], TN) for x, y in zip(left, right))
        for c in range(own_ref.shape[0]):
            low, high = value[2 * c * r : 2 * c * r + r], value[2 * c * r + r : 2 * c * r + 2 * r]
            own_ref[c] = jnp.where(first, low, high).astype(BF)
            other_ref[c] = jnp.where(first, high, low).astype(BF)


def wgrad(pos, pairs, nf, waits=()):
    flat = lambda x: x.reshape(-1, x.shape[-1])
    pairs = [([flat(x) for x in a], [flat(x) for x in b]) for a, b in pairs]
    m = pairs[0][0][0].shape[1]
    r = m // nf
    cuts = []
    for i, (_, right) in enumerate(pairs):
        width = right[0].shape[1]
        cuts += [(i, a, min(a + 1152, width)) for a in range(0, width, 1152)]
    ins = [x for a, b in pairs for x in a + b]
    shapes = [((nf // 2, r, b - a), BF) for _, a, b in cuts]
    vmem = pl.BlockSpec(memory_space=pltpu.VMEM)
    outs = call(
        partial(wgrad_kernel, pairs=[(len(a), len(b)) for a, b in pairs], cuts=cuts, r=r),
        (pos, *ins),
        [smem()] + [vmem] * len(ins),
        shapes * 2,
        [vmem] * (2 * len(cuts)),
        waits=waits,
        vmem=40 << 20,
    )
    return list(outs[: len(cuts)]), list(outs[len(cuts) :])


def vectors_kernel(pos_ref, sums_ref, a_ref, gate_ref, qkv_ref, xv_ref, fed_ref, *refs, parts, r):
    hiddens, (own_ref, other_ref, all_ref) = refs[:-3], refs[-3:]
    sp = pos_ref[0]
    all_ref[...] = jnp.zeros_like(all_ref)
    sums, a_sums = jnp.sum(sums_ref[...], axis=0), jnp.sum(a_ref[...], axis=0)
    qkv = jnp.sum(qkv_ref[...], axis=0)
    own = qkv.shape[1] // 3

    def spread(row, value):
        for i in range(2):
            all_ref[row : row + 1, i * own : (i + 1) * own] = jnp.where(sp == i, value, 0.0)

    spread(0, qkv[:, :own])
    spread(1, qkv[:, 2 * own :])
    spread(4, xv_ref[...])
    fed = jnp.sum(fed_ref[...], axis=0)
    gate = jnp.sum(gate_ref[...], axis=0)
    rows = {2: sums[5:6], 3: sums[4:5], 5: sums[3:4], 6: fed, 7: a_sums[0:1], 8: a_sums[1:2]}
    rows |= {9: sums[2:3], 10: sums[0:1], 11: sums[1:2], 12: gate}
    for row, value in rows.items():
        all_ref[row : row + 1] = value
    hidden = sum(jnp.sum(h[...], axis=0) for h in hiddens)
    pw = hidden.shape[1] // parts
    for i in range(2):
        for j in range(parts):
            row = 13 + i * parts + j
            all_ref[row : row + 1] = jnp.where(sp == i, hidden[:, j * pw : (j + 1) * pw], 0.0)
    columns = all_ref[...].T
    first = pos_ref[1] == 0
    for c in range(own_ref.shape[0]):
        low, high = columns[2 * c * r : 2 * c * r + r], columns[2 * c * r + r : 2 * c * r + 2 * r]
        own_ref[c] = jnp.where(first, low, high).astype(BF)
        other_ref[c] = jnp.where(first, high, low).astype(BF)


def vector_halves(pos, sums, a_sums, gate, qkv, xv, fed, hiddens, parts, nf, waits=()):
    d = sums.shape[2]
    ins = (pos, sums, a_sums, gate, qkv, xv, fed, *hiddens)
    vmem = pl.BlockSpec(memory_space=pltpu.VMEM)
    return call(
        partial(vectors_kernel, parts=parts, r=d // nf),
        ins,
        [smem()] + [vmem] * (len(ins) - 1),
        [((nf // 2, d // nf, 128), BF)] * 2,
        [vmem] * 2,
        scratch=[pltpu.VMEM((128, d), F32)],
        waits=waits,
        vmem=16 << 20,
    )


def last_out_kernel(pos_ref, x_ref, got_ref, kv_ref, in_ref, table_ref, expand_ref, *vec_refs):
    first = pos_ref[0] == 0
    own = kv_ref.shape[1] // 4
    for p in range(5):
        x, got = x_ref[:, p * own : (p + 1) * own].astype(F32), got_ref[:, p * own : (p + 1) * own].astype(F32)
        ref, at = (kv_ref, p) if p < 2 else (in_ref, p - 2)
        ref[:, 2 * at * own : (2 * at + 1) * own] = jnp.where(first, x, got)
        ref[:, (2 * at + 1) * own : (2 * at + 2) * own] = jnp.where(first, got, x)
    vectors = (x_ref[:, 5 * own :].astype(F32) + got_ref[:, 5 * own :].astype(F32)).T
    for i, ref in enumerate(vec_refs):
        ref[...] = vectors[i : i + 1]
    table_ref[...] = vectors[7:13]
    expand_ref[...] = vectors[13 : 13 + expand_ref.shape[0]]


def last_outputs(pos, x, own, expands):
    vmem = pl.BlockSpec(memory_space=pltpu.VMEM)
    r = x.shape[0]
    return call(
        last_out_kernel,
        (pos, x, swap(x)),
        [smem()] + [vmem] * 2,
        [((r, 4 * own), F32), ((r, 6 * own), F32), ((6, r), F32), ((expands, r), F32)] + [((1, r), F32)] * 7,
        [vmem] * 11,
        vmem=16 << 20,
    )


def ff_out_kernel(pos_ref, x_ref, got_ref, c_ref, e_ref, *, parts, nf):
    first = pos_ref[0] == 0
    r, d = x_ref.shape[0], c_ref.shape[1]
    for i in range(2):
        for j in range(parts):
            cols = slice(j * d, (j + 1) * d)
            value = jnp.where(first == (i == 0), x_ref[:, cols], got_ref[:, cols])
            c_ref[(i * parts + j) * r : (i * parts + j + 1) * r] = value.astype(F32)
    for j in range(parts):
        cols = slice((parts + j) * d, (parts + j + 1) * d)
        x, got = x_ref[:, cols].astype(F32), got_ref[:, cols].astype(F32)
        low, high = jnp.where(first, x, got), jnp.where(first, got, x)
        for f in range(nf):
            at = f * 2 * parts * r + j * r
            e_ref[:, at : at + r] = low[:, f * r : (f + 1) * r]
            e_ref[:, at + parts * r : at + parts * r + r] = high[:, f * r : (f + 1) * r]


def ff_outputs(pos, x, parts, d, nf, waits=()):
    vmem = pl.BlockSpec(memory_space=pltpu.VMEM)
    r = x.shape[0]
    return call(
        partial(ff_out_kernel, parts=parts, nf=nf),
        (pos, x, swap(x)),
        [smem()] + [vmem] * 2,
        [((2 * parts * r, d), F32), ((r, 2 * parts * d), F32)],
        [vmem] * 2,
        waits=waits,
        vmem=16 << 20,
        token=True,
    )


def core_sum_kernel(pos_ref, *refs, pieces):
    owns, gots, (y_ref, other_ref) = refs[:pieces], refs[pieces : 2 * pieces], refs[2 * pieces :]
    first = pos_ref[2] == 0
    at = 0
    for own, got in zip(owns, gots):
        cols = slice(at, at + own.shape[2])
        low = own[0].astype(F32) + got[0].astype(F32)
        high = own[1].astype(F32) + got[1].astype(F32)
        y_ref[0, :, cols] = jnp.where(first, low, high).astype(BF)
        other_ref[0, :, cols] = jnp.where(first, high, low).astype(BF)
        at += own.shape[2]


def y_sum_kernel(pos_ref, own_ref, got_ref, *outs):
    nz = len(outs)
    for d in range(nz):
        at = lax.rem(pos_ref[3] + d, nz)
        outs[d][...] = (own_ref[at].astype(F32) + got_ref[at].astype(F32)).astype(BF)


def z_sum_kernel(*refs):
    refs[-1][...] = sum(x[...].astype(F32) for x in refs[:-1]).astype(BF)


def in_vmem(kernel, ins, outs, waits=()):
    spec = pl.BlockSpec(memory_space=pltpu.VMEM)
    specs = [smem() if x.dtype == jnp.int32 else spec for x in ins]
    return call(kernel, ins, specs, [(s, BF) for s in outs], [spec] * len(outs), waits=waits, vmem=16 << 20)


def shift_z(x, nf, d):
    return lax.ppermute(x, "fsdp", [(i, (i + 4 * d) % nf) for i in range(nf)])


def cross_y(x, nf):
    return lax.ppermute(x, "fsdp", [(i, i ^ 2) for i in range(nf)])


def cross_core(x, nf):
    return lax.ppermute(x, "fsdp", [(i, i ^ 1) for i in range(nf)])


def sum_core(pos, owns, others, nf, waits=()):
    r, w = owns[0].shape[1], sum(x.shape[2] for x in owns)
    two = [pl.BlockSpec((2,) + x.shape[1:], lambda i: (i, 0, 0)) for x in owns]
    one = pl.BlockSpec((1, r, w), lambda i: (i, 0, 0))
    return call(
        partial(core_sum_kernel, pieces=len(owns)),
        (pos, *owns, *[cross_core(x, nf) for x in others]),
        [smem(), *two, *two],
        [((nf // 4, r, w), BF)] * 2,
        [one, one],
        grid=(nf // 4,),
        waits=waits,
        vmem=16 << 20,
    )


def sum_y(pos, mine, other, nf, waits=()):
    nz, r, w = mine.shape
    return in_vmem(y_sum_kernel, (pos, mine, cross_y(other, nf)), [(r, w)] * nz, waits)


def sum_z(chunks, nf, waits=()):
    got = [shift_z(chunks[d], nf, d) for d in range(1, len(chunks))]
    return in_vmem(z_sum_kernel, (chunks[0], *got), [chunks[0].shape], waits)[0]


def swap(x):
    return lax.ppermute(x, "sp", [(0, 1), (1, 0)])


def pick(x, index, axis):
    return lax.dynamic_index_in_dim(x, index, axis, keepdims=False)


def in_order(own, other, index, axis=-1):
    return jnp.where(
        index == 0, jnp.concatenate([own, other], axis=axis), jnp.concatenate([other, own], axis=axis)
    )


def halves(x, index, axis=-1):
    low, high = jnp.split(x, 2, axis=axis)
    return jnp.where(index == 0, low, high), jnp.where(index == 0, high, low)


def gather_tokens(x, nsp):
    if nsp == 2:
        return [x, swap(x)]
    return [lax.all_gather(x, "sp", axis=1, tiled=True)]


def scatter_tokens(parts, nsp):
    if nsp == 2:
        return parts[0], swap(parts[1])
    total = lax.psum_scatter(parts[0], "sp", scatter_dimension=1, tiled=True)
    return total, jnp.zeros_like(total)


def heads_to_tokens(x, nsp, index, others):
    if nsp == 2:
        half = x.shape[1] // 2
        return in_order(x[:, :half], after(swap(x[:, half:]), *others), index)
    return lax.all_to_all(x, "sp", split_axis=1, concat_axis=2, tiled=True)


def tokens_to_heads(parts, nsp):
    if nsp == 2:
        return [parts[0], swap(parts[1])]
    return [lax.all_to_all(parts[0], "sp", split_axis=2, concat_axis=1, tiled=True)]


def gather_axis(x, nsp, index, axis):
    if nsp == 2:
        return in_order(x, swap(x), index, axis)
    return lax.all_gather(x, "sp", axis=axis, tiled=True)


def scatter_axis(x, nsp, index, axis):
    if nsp == 2:
        own, other = halves(x, index, axis)
        return own.astype(F32) + swap(other.astype(BF)).astype(F32)
    return lax.psum_scatter(x.astype(BF), "sp", scatter_dimension=axis, tiled=True).astype(F32)


def sum_sp(x, nsp):
    if nsp == 2:
        return x.astype(F32) + swap(x).astype(F32)
    return lax.psum(x, "sp").astype(F32)


def gather_sp(x, nsp, index):
    if nsp == 2:
        got = swap(x)
        return [jnp.where(index == 0, x, got).astype(F32), jnp.where(index == 0, got, x).astype(F32)]
    return list(lax.all_gather(x, "sp").astype(F32))


def merge_sp(x, sums, gathers, nsp, index):
    (a, b), (c, d) = sums[0], gathers[0]
    if nsp == 2:
        got = swap(x)
        total = x[:, a:b].astype(F32) + got[:, a:b].astype(F32)
        x, got = x[:, c:d].astype(F32), got[:, c:d].astype(F32)
        return total, [jnp.where(index == 0, x, got), jnp.where(index == 0, got, x)]
    return lax.psum(x[:, a:b].astype(F32), "sp"), list(lax.all_gather(x[:, c:d], "sp").astype(F32))


def copy_kernel(at_ref, *refs, n, dim):
    ins, out, sems = refs[:n], refs[n], refs[n + 1]
    copies = []
    for i in range(n):
        index = (slice(None),) * dim + (at_ref[i],)
        copies.append(pltpu.make_async_copy(ins[i], out.at[index], sems.at[i]))
    for c in copies:
        c.start()
    for c in copies:
        c.wait()


def place_all(parts, at, dim, waits=()):
    n = len(parts)
    shape = parts[0].shape[:dim] + (n,) + parts[0].shape[dim:]
    return call(
        partial(copy_kernel, n=n, dim=dim),
        (at, *parts),
        [smem()] + anywhere(n),
        [(shape, parts[0].dtype)],
        [pl.BlockSpec(memory_space=pltpu.VMEM)],
        scratch=[pltpu.SemaphoreType.DMA((n,))],
        waits=waits,
        vmem=24 << 20,
    )[0]


def after(x, *others):
    return lax.optimization_barrier((x, *others))[0]


def column_sum(x):
    return jnp.sum(x, axis=(0, 1), dtype=F32)


def linear(x, w):
    return jnp.einsum("lsd,de->lse", x, w, preferred_element_type=F32)


def linear_back(x, w):
    return jnp.einsum("lse,de->lsd", x, w, preferred_element_type=F32)


def on_device(
    latent_tokens,
    caption_tokens,
    caption_len,
    time_embed,
    mod_table,
    self_input_weight,
    self_query_bias,
    self_value_bias,
    self_output_weight,
    self_output_bias,
    cross_query_weight,
    cross_query_bias,
    cross_keyval_weight,
    cross_value_bias,
    cross_output_weight,
    cross_output_bias,
    expand_weight,
    expand_bias,
    contract_weight,
    contract_bias,
    out_grad,
):
    nsp, nf = lax.axis_size("sp"), lax.axis_size("fsdp")
    sp, fsdp = lax.axis_index("sp"), lax.axis_index("fsdp")
    core, y, z, nz = fsdp % 2, (fsdp // 2) % 2, fsdp // 4, nf // 4
    pos = jnp.stack([sp, core, y, z]).astype(jnp.int32)
    latents, local_len, width = latent_tokens.shape
    rows = width // nf
    own = width // nsp
    hidden_rows = contract_weight.shape[0]
    hidden_own = hidden_rows // nsp
    parts = max(1, hidden_own // rows)
    block = hidden_own // parts
    part_width = nf * block

    def columns(w, pieces, groups=1):
        size = w.shape[1] // pieces // nsp // groups
        out = []
        for i in range(nsp):
            starts = [
                p * size * nsp * groups + (i * groups + g) * size for g in range(groups) for p in range(pieces)
            ]
            out.append(jnp.concatenate([w[:, a : a + size] for a in starts], axis=1))
        if nsp == 2:
            return jnp.where(sp == 0, out[0], out[1])
        return pick(jnp.stack(out), sp, 0)

    small = jnp.concatenate(
        [
            jnp.stack(
                [
                    self_query_bias,
                    self_value_bias,
                    self_output_bias,
                    cross_query_bias,
                    cross_value_bias,
                    cross_output_bias,
                    contract_bias,
                ]
            ),
            mod_table,
            expand_bias.reshape(-1, rows),
        ],
        axis=0,
    )
    smalls = small.shape[0]
    small = jnp.pad(small.T, ((0, 0), (0, 128 - smalls)))

    stream_swap = gather_tokens(latent_tokens, nsp)

    grads = gather_tokens(out_grad, nsp)
    caption_all = gather_axis(caption_tokens, nsp, sp, 1)
    stream_all = jnp.concatenate(stream_swap, axis=1)
    first = jnp.concatenate([columns(self_input_weight, 3), small], axis=1)
    second = jnp.concatenate(
        [self_output_weight, cross_query_weight, cross_output_weight, columns(cross_keyval_weight, 2)], axis=1
    )
    last = pick(expand_weight.reshape(rows, nf, nsp, parts, block), sp, 2)
    last = last.transpose(0, 2, 1, 3).reshape(rows, parts * part_width)
    contract_shard = pick(contract_weight.reshape(nsp, parts, block, width), sp, 0)
    if block == rows:
        last = jnp.concatenate([last] + [contract_shard[j] for j in range(parts)], axis=1)

    second = lax.all_gather(second, "fsdp", axis=0, tiled=True)
    ring = [first] + [shift_z(first, nf, d) for d in range(1, nz)]
    across = [cross_y(x, nf) for x in ring]
    at = jnp.stack([((z - d) % nz) * 2 + y for d in range(nz)] + [((z - d) % nz) * 2 + 1 - y for d in range(nz)])
    mine = place_all(ring + across, at.astype(jnp.int32), 0, (stream_all, last, caption_all))
    first = place_all([mine, cross_core(mine, nf)], jnp.stack([core, 1 - core]).astype(jnp.int32), 1)
    first = first.reshape(width, -1)
    whole_expand = lax.all_gather(after(last, mine), "fsdp", axis=0, tiled=True)
    if block == rows:
        whole_contracts = [(whole_expand, parts * part_width // width + j) for j in range(parts)]
    else:
        contract_shard = lax.all_gather(after(contract_shard[0], mine), "fsdp", axis=0, tiled=True)
        whole_contracts = [(contract_shard, 0)]

    smalls_all = first[:, 3 * own :].astype(F32).T

    def own_part(v):
        return pick(v.reshape(nsp, own), sp, 0)

    bias_query, bias_value = own_part(smalls_all[0]), own_part(smalls_all[1])
    bias_qkv = jnp.concatenate([bias_query, jnp.zeros_like(bias_query), bias_value]).reshape(1, 3 * own)
    vecs = smalls_all[:8]
    bias_xvalue = own_part(smalls_all[4])
    bias_expand = smalls_all[13:smalls].reshape(-1, nf, rows).transpose(1, 0, 2).reshape(nf, nsp, parts, block)
    bias_expand = pick(bias_expand, sp, 1).transpose(1, 0, 2).reshape(parts * part_width)
    mods = smalls_all[7:13][None] + time_embed.reshape(latents, 6, width)
    mods = jnp.pad(mods, ((0, 0), (0, 2), (0, 0)))

    norm_a, qkv = qkv_forward(stream_all, mods, bias_qkv, first, 3 * own)

    mixed, lse = self_forward(qkv, tuple(grads[1:]))
    second = after(second, mixed)
    whole_keyval = second[:, 3 * width :]

    keyval = linear(caption_all, whole_keyval)
    cross_keys = gather_axis(keyval[..., :own].astype(BF), nsp, sp, 2)
    cross_values = gather_axis((keyval[..., own:] + bias_xvalue).astype(BF), nsp, sp, 2)
    mixed_tokens = after(heads_to_tokens(mixed, nsp, sp, (cross_keys, cross_values)), mixed)
    place = jnp.arange(caption_all.shape[1])
    mask = jnp.where(place[None] < caption_len[:, None], 0.0, NEG).astype(F32)[..., None]
    attended, attn_low, cross_queries, cross_lse, cross_mixed, after_cross, norm_b = middle_forward(
        mixed_tokens, latent_tokens, mods, vecs, second, cross_keys, cross_values, mask
    )

    norm_bs = gather_tokens(norm_b, nsp)
    ff_out = [None] * len(norm_bs)
    waits = ()
    for c in reversed(range(len(norm_bs))):
        ff_out[c] = feed_forward(norm_bs[c], grads[c], mods, whole_expand, whole_contracts, bias_expand, waits)
        waits = (ff_out[c][3],)
    acts, hidden_grads, fed_grads, norm_b_grads, hidden_sums, fed_sums = zip(*ff_out)
    norm_b_terms = scatter_tokens(norm_b_grads, nsp)
    expand_bgrad = sum(jnp.sum(x, axis=(0, 1)) for x in hidden_sums)
    if nsp == 2:
        contract_bgrad = jnp.sum(fed_sums[0], axis=(0, 1))
    else:
        contract_bgrad = column_sum(mods[:, 5:6] * out_grad.astype(F32))
    if block == rows:
        ff_own = columns_wgrad(acts, fed_grads, True, 2 * parts * width, 0)
        ff_own = columns_wgrad(norm_bs, hidden_grads, False, 2 * parts * width, parts, ff_own, (norm_b_terms[1],))
        ff_done = ff_own
        ff_own = lax.psum_scatter(ff_own, "fsdp", scatter_dimension=0, tiled=True)
        ff_sp = gather_sp(ff_own, nsp, sp)
        contract_sp, expand_sp = [g[:, : parts * width] for g in ff_sp], [g[:, parts * width :] for g in ff_sp]
    else:
        contract_own = jnp.einsum("lsd,lse->de", acts[0], fed_grads[0], preferred_element_type=F32).astype(BF)
        expand_own = jnp.einsum("lsd,lse->de", norm_bs[0], hidden_grads[0], preferred_element_type=F32).astype(BF)
        ff_done = expand_own
        contract_sp = gather_sp(lax.psum_scatter(contract_own, "fsdp", scatter_dimension=0, tiled=True), nsp, sp)
        expand_sp = gather_sp(lax.psum_scatter(expand_own, "fsdp", scatter_dimension=0, tiled=True), nsp, sp)

    crossed_grad, xquery_grad, attended_grad, attn_stream_grad, sums, *rest = middle_backward(
        pos, *norm_b_terms, after_cross, out_grad, mods, second, cross_keys, cross_values, mask,
        cross_queries, cross_lse, attended, nsp, waits=(ff_done,),
    )
    shift_b_grad, scale_b_grad, gate_a_grad = sums[:, 0], sums[:, 1], sums[:, 2]
    tokens_grads, keyval_parts = rest[: len(rest) // 2], rest[len(rest) // 2 :]
    mixed_grads = tokens_to_heads(tokens_grads, nsp)
    feds, gate_b_grad = fed_forward(
        acts, grads, whole_contracts, vecs, width, 1.0 if nsp == 2 else 1.0 / nsp, (attended_grad,)
    )
    fed_terms = scatter_tokens(feds, nsp)
    if nsp == 2:
        keyval_grad = (keyval_parts[0].astype(F32) + swap(keyval_parts[1]).astype(F32)).astype(BF)
    else:
        dk, dv = jnp.split(keyval_parts[0], 2, axis=-1)
        keyval_grad = jnp.concatenate([scatter_axis(dk, nsp, sp, 2), scatter_axis(dv, nsp, sp, 2)], axis=-1)
        keyval_grad = keyval_grad.astype(BF)
    outer_halves = wgrad(
        pos,
        [([attn_low], [xquery_grad]), ([cross_mixed], [crossed_grad]), ([mixed_tokens], [attended_grad])],
        nf,
        (feds[0], mixed_grads[-1], keyval_grad),
    )
    outer_core = sum_core(pos, *outer_halves, nf)
    caption_grad = scatter_axis(linear_back(keyval_grad, whole_keyval), nsp, sp, 1)
    xvalue_bgrad = column_sum(keyval_grad[..., own:])

    projected_grad = self_backward(qkv, mixed_grads, lse, (outer_core[0],))
    input_out = input_backward(projected_grad, stream_swap, first)
    norm_a_terms = scatter_tokens(list(input_out[:-2]), nsp)
    shift_a_grad, scale_a_grad = input_out[-2][:, 0], input_out[-2][:, 1]
    if nsp == 2 and block == rows:
        vector_parts = vector_halves(
            pos, sums, input_out[-2], gate_b_grad[:, None], input_out[-1], xvalue_bgrad[None], fed_sums[0],
            hidden_sums, parts, nf,
        )
    else:

        def spread(x):
            return jnp.where(jnp.arange(nsp)[:, None] == sp, x[None], 0.0).reshape(nsp * x.shape[0])

        qkv_bgrad = column_sum(input_out[-1])
        expand_bias_part = jnp.where(
            jnp.arange(nsp)[None, :, None, None] == sp,
            expand_bgrad.reshape(parts, nf, block).transpose(1, 0, 2)[:, None],
            0.0,
        ).reshape(nf, -1, rows)
        vectors = jnp.stack(
            [
                spread(qkv_bgrad[:own]),
                spread(qkv_bgrad[2 * own :]),
                jnp.sum(sums[:, 5], axis=0),
                jnp.sum(sums[:, 4], axis=0),
                spread(xvalue_bgrad),
                jnp.sum(sums[:, 3], axis=0),
                contract_bgrad,
                jnp.sum(shift_a_grad, axis=0),
                jnp.sum(scale_a_grad, axis=0),
                jnp.sum(gate_a_grad, axis=0),
                jnp.sum(shift_b_grad, axis=0),
                jnp.sum(scale_b_grad, axis=0),
                jnp.sum(gate_b_grad, axis=0),
            ]
        )
        vectors = jnp.concatenate([vectors, expand_bias_part.transpose(1, 0, 2).reshape(-1, width)])
        vectors = jnp.pad(vectors.T, ((0, 0), (0, 128 - vectors.shape[0]))).astype(BF)
        vectors = vectors.reshape(nf // 2, 2, rows, 128)
        vector_parts = (pick(vectors, core, 1), pick(vectors, 1 - core, 1))
    count = 13 + hidden_rows // rows
    input_own, input_other = wgrad(
        pos, [([caption_all], [keyval_grad]), ([norm_a], [projected_grad])], nf, (vector_parts[0], fed_terms[1])
    )
    outer_y = sum_y(pos, *outer_core, nf, waits=(input_own[0],))
    input_core = sum_core(
        pos, input_own + [vector_parts[0]], input_other + [vector_parts[1]], nf, waits=(outer_y[0],)
    )
    embed_part = jnp.stack(
        [shift_a_grad, scale_a_grad, gate_a_grad, shift_b_grad, scale_b_grad, gate_b_grad], axis=1
    )
    time_grad = sum_sp(embed_part.reshape(latents, 6 * width), nsp)
    outer_own = sum_z(outer_y, nf, waits=(input_core[0], norm_a_terms[1], time_grad))
    input_y = sum_y(pos, *input_core, nf, waits=(outer_own,))
    latent_grad, *tokens = last_backward(*norm_a_terms, latent_tokens, mods, attn_stream_grad, (input_y[0],))
    block_out, token = finish_forward(*fed_terms, after_cross, mods, vecs, waits=(input_y[0],))
    tokens.append(token)

    if nsp == 2 and block == rows:
        contract_out, expand_out, token = ff_outputs(pos, ff_own, parts, width, nf, (input_y[0],))
        tokens.append(token)
    else:
        contract_out = jnp.concatenate(
            [
                g[:, j * width : (j + 1) * width]
                for g in contract_sp
                for j in range(contract_sp[0].shape[1] // width)
            ],
            axis=0,
        )
        expand_out = jnp.stack(
            [g.reshape(rows, parts, nf, block).transpose(0, 2, 1, 3) for g in expand_sp], axis=2
        ).reshape(rows, -1)
    outer_sum = sum_sp(outer_own, nsp)
    xquery_out, xoutput_out, output_out = [outer_sum[:, i * width : (i + 1) * width] for i in range(3)]
    input_own = sum_z(input_y, nf, waits=tuple(tokens))
    if nsp == 2:
        keyval_out, input_wout, table_out, expand_bout, *owned = last_outputs(pos, input_own, own, count - 13)
        owned = [x.reshape(rows) for x in owned]
        expand_bout = expand_bout.reshape(hidden_rows)
    else:
        inputs = list(lax.all_gather(input_own[:, : 5 * own], "sp").astype(F32))
        keyval_out = jnp.concatenate([g[:, p * own : (p + 1) * own] for p in range(2) for g in inputs], axis=1)
        input_wout = jnp.concatenate([g[:, p * own : (p + 1) * own] for p in range(2, 5) for g in inputs], axis=1)
        owned = sum_sp(input_own[:, 5 * own :], nsp)[:, :count].T
        expand_bout = owned[13:count].reshape(hidden_rows)
        table_out = owned[7:13]
    return (
        block_out,
        latent_grad,
        caption_grad,
        time_grad,
        table_out,
        input_wout,
        owned[0],
        owned[1],
        output_out,
        owned[2],
        xquery_out,
        owned[3],
        keyval_out,
        owned[4],
        xoutput_out,
        owned[5],
        expand_out,
        expand_bout,
        contract_out,
        owned[6],
    )


def solution(mesh):
    row, vec, tokens = P("fsdp", None), P("fsdp"), P("fsdp", "sp", None)
    in_specs = (
        (tokens, tokens, vec, row, P(None, "fsdp"), row, vec, vec)
        + (row, vec) * 2
        + (row, vec) * 4
        + (tokens,)
    )
    out_specs = (
        (tokens, tokens, tokens, row, P(None, "fsdp"), row, vec, vec) + (row, vec) * 2 + (row, vec) * 4
    )
    return jax.shard_map(
        on_device, mesh=mesh, in_specs=in_specs, out_specs=out_specs, check_vma=False
    )
```
